128 devices in a mesh: ctx: 16 (over y_lo, x, core), tp: 8 (over y_hi, z).
Axes of the slice: x: 4, y: 4 (y_hi: 2, y_lo: 2; y = y_hi * 2 + y_lo), z: 4, core: 2. Of those that a mesh axis runs over, the one named last changes fastest.
Arguments:
- stretch_start: int32 [1], replicated, may hold values from 8192 to 16384
- stretch_q: bfloat16 [2048, 8192], P('ctx', 'tp'), may hold values from -9 to 9
- stretch_k: bfloat16 [2048, 1024], P('ctx', 'tp'), may hold values from -6 to 6
- stretch_v: bfloat16 [2048, 1024], P('ctx', 'tp'), may hold values from -36 to 36
- prefix_k: bfloat16 [16384, 1024], P('ctx', 'tp'), may hold values from -6 to 6
- prefix_v: bfloat16 [16384, 1024], P('ctx', 'tp'), may hold values from -36 to 36
- dec_len: int32 [64], P('ctx'), may hold values from 1 to 2048
- dec_q: bfloat16 [64, 8192], P('ctx', 'tp'), may hold values from -9 to 9
- dec_k: bfloat16 [64, 1024], P('ctx', 'tp'), may hold values from -6 to 6
- dec_v: bfloat16 [64, 1024], P('ctx', 'tp'), may hold values from -36 to 36
- cache_k: bfloat16 [64, 2048, 1024], P('ctx', None, 'tp'), may hold values from -6 to 6
- cache_v: bfloat16 [64, 2048, 1024], P('ctx', None, 'tp'), may hold values from -36 to 36
- hand_owner: int32 [256, 1], P('ctx'), may hold values from 0 to 15; in each aligned block of 16 rows (0 to 15, 16 to 31, ...) at most 2 rows name the same one
- hand_count: int32 [256], P('ctx'), may hold values from 1 to 128
- hand_q: bfloat16 [256, 8192], P('ctx', 'tp'), may hold values from -9 to 9
- hand_k: bfloat16 [256, 128, 1024], P('ctx', None, 'tp'), may hold values from -6 to 6
- hand_v: bfloat16 [256, 128, 1024], P('ctx', None, 'tp'), may hold values from -36 to 36
- out_weight: bfloat16 [8192, 8192], P('tp'), may hold values from -0.0625 to 0.0625
Outputs:
- stretch_out: bfloat16 [2048, 8192], P('ctx', 'tp')
- dec_out: bfloat16 [64, 8192], P('ctx', 'tp')
- new_out: bfloat16 [512, 8192], P('ctx', 'tp')
The draws below stay inside these ranges and needn't reach their ends.
Inputs may be any that keep to these rules, and one draw needn't show every extreme that they name: `hand_owner`: among the 16 blocks of one index of ctx (aligned blocks of rows) no owner is named more than 2 times.
All inputs are finite; a program needn't handle non-finite values.
Results may differ from the reference program's by a relative error of at most 0.015.
Values may be sent and summed in bfloat16 or wider, within the bound.
No kernel may reach another device: no remote copies, remote signals or barrier semaphores. Data moves between devices by JAX's collectives and lax.ppermute only.
A program may use at most 256 MiB of HBM per device.

```python
import math
import jax
import jax.numpy as jnp
import numpy as np
from jax import lax

D = 8192
HEADS = 64
KV_HEADS = 8
HEAD_DIM = 128
CACHE = 2048
BLK = 128
FIN_DEV = 16
MOST = 2
STRETCH = 2048
PREFIX = 16384
DROWS = 64
NBLK = 256
SLOTS = 32
NEW_ROWS = 512
N_CTX = 16


def drawn_keys(key, rows, width):
    drawn = jnp.clip(jax.random.normal(key, (rows, width), jnp.float32), -6.0, 6.0)
    return drawn


def drawn_queries(key, rows, width):
    drawn = jnp.clip(1.5 * jax.random.normal(key, (rows, width), jnp.float32), -9.0, 9.0)
    return drawn


def draw_stretch_q(key, part):
    key = jax.random.fold_in(key, 11)
    return drawn_queries(key, STRETCH, HEADS * HEAD_DIM).astype(jnp.bfloat16)


def draw_dec_q(key, part):
    key = jax.random.fold_in(key, 12)
    return drawn_queries(key, DROWS, HEADS * HEAD_DIM).astype(jnp.bfloat16)


def draw_hand_q(key, part):
    key = jax.random.fold_in(key, 13)
    return drawn_queries(key, NBLK, HEADS * HEAD_DIM).astype(jnp.bfloat16)


def draw_stretch_k(key, part):
    key = jax.random.fold_in(key, 21)
    return drawn_keys(key, STRETCH, KV_HEADS * HEAD_DIM).astype(jnp.bfloat16)


def draw_prefix_k(key, part):
    key = jax.random.fold_in(key, 22)
    return drawn_keys(key, PREFIX, KV_HEADS * HEAD_DIM).astype(jnp.bfloat16)


def draw_cache_k(key, part):
    key = jax.random.fold_in(key, 23)
    flat = drawn_keys(key, DROWS * CACHE, KV_HEADS * HEAD_DIM)
    return flat.reshape(DROWS, CACHE, KV_HEADS * HEAD_DIM).astype(jnp.bfloat16)


def draw_hand_k(key, part):
    key = jax.random.fold_in(key, 24)
    flat = drawn_keys(key, NBLK * BLK, KV_HEADS * HEAD_DIM)
    return flat.reshape(NBLK, BLK, KV_HEADS * HEAD_DIM).astype(jnp.bfloat16)


def draw_dec_len(key, part):
    key = jax.random.fold_in(key, 31)
    lengths = jax.random.randint(jax.random.fold_in(key, 1), (DROWS,), 1, CACHE + 1, jnp.int32)
    chosen = jax.random.randint(jax.random.fold_in(key, 2), (), 0, DROWS, jnp.int32)
    return lengths.at[chosen].set(CACHE)


def plant(result, stream_key, low, largest):
    extent = result.shape
    spot = [jax.random.randint(jax.random.fold_in(stream_key, axis), (), 0, extent[axis]) for axis in range(len(extent))]
    result = result.at[tuple(spot)].set(low)
    longest = extent.index(max(extent))
    spot[longest] = (spot[longest] + 1) % extent[longest]
    return result.at[tuple(spot)].set(largest)


def levels(own_key, dims, pieces, low, largest):
    level = 1.0
    for axis_at, blocks in pieces:
        heights = jax.random.uniform(jax.random.fold_in(jax.random.fold_in(own_key, 6), axis_at), (blocks,), jnp.float32, low / len(pieces), largest / len(pieces))
        level = level * jnp.repeat(jnp.exp(heights), dims[axis_at] // blocks).reshape((-1,) + (1,) * (len(dims) - 1 - axis_at))
    return level


def routed_block(rng, own, number, rows, number_of, top, limit, slope):
    sequence = jax.random.permutation(rng, number_of)
    heavy_load, usual = load_shares(number_of, rows * top, limit, slope, True), load_shares(number_of, rows * top, limit, slope, False)
    places = jnp.arange(number_of)

    def named(sizes, rotation):
        used = int((sizes > 0).sum())
        fixed = max(1, used // 4)
        moved = fixed + (places - fixed + rotation * (used - fixed)) % max(1, number_of - fixed)
        return jnp.zeros((number_of,), jnp.int32).at[sequence[jnp.where(places < fixed, places, moved)]].set(jnp.asarray(sizes, jnp.int32))

    sizes = jnp.where(number % 4 == 0, named(heavy_load, number // 4), named(usual, number - number // 4 - 1))
    mixed = jax.random.permutation(jax.random.fold_in(own, 3), number_of)
    donor, sink = mixed[0:number_of // 2 * 2:2], mixed[1:number_of // 2 * 2:2]
    margin = jnp.minimum(sizes[donor] - 1, limit - sizes[sink]) // 2
    margin = jnp.where((donor == sequence[0]) | (sink == sequence[0]) | (sizes[sink] == 0), 0, jnp.maximum(margin, 0))
    moved = jax.random.randint(jax.random.fold_in(own, 4), (number_of // 2,), 0, 1 << 20) % (margin + 1)
    sizes = sizes.at[donor].add(-moved).at[sink].add(moved)
    labels = jnp.searchsorted(jnp.cumsum(sizes), jnp.arange(rows * top), side="right").astype(jnp.int32)
    table = labels.reshape(top, rows).T
    table = table[jax.random.permutation(jax.random.fold_in(own, 1), rows)]
    rotation = jax.random.randint(jax.random.fold_in(own, 2), (rows, 1), 0, top)
    return jnp.take_along_axis(table, (jnp.arange(top)[None, :] + rotation) % top, axis=1)


def load_shares(amount, total, most, slope, full):
    weights = [(1 << 20) // math.isqrt(standing ** slope) + 1 for standing in range(1, amount + 1)]
    largest = most if full else min(most, max(-(-total // amount), total * weights[0] // sum(weights)))
    least = 1 if total - largest >= amount - 1 else 0
    given, surplus = [largest] + [least] * (amount - 1), total - largest - least * (amount - 1)
    while surplus > 0:
        free = [i for i in range(1, amount) if given[i] < largest] or [i for i in range(1, amount) if given[i] < most]
        mass, remaining = sum([weights[i] for i in free]), surplus
        for i in free:
            more = min(most - given[i], max(1, remaining * weights[i] // mass), surplus)
            given[i] = given[i] + more
            surplus = surplus - more
    return np.array(given)


def bell_draw(key, shape, deviation, limit, pieces=(), kind=jnp.bfloat16):
    gain = levels(key, shape, pieces, -0.22, 0.18) if pieces else 1.0
    result = jax.random.normal(key, shape, jnp.float32) * deviation * gain
    return jnp.minimum(jnp.maximum(result, -limit), limit).astype(kind)


def setup_inputs(seed: int = 0) -> dict:
    arg_keys = jax.random.split(jax.random.key(seed), 19)
    stretch_start = jax.random.randint(arg_keys[0], (1,), PREFIX // 2, PREFIX + 1).astype(jnp.int32)
    stretch_q = draw_stretch_q(jax.random.fold_in(arg_keys[18], 71), 0)
    stretch_k = draw_stretch_k(jax.random.fold_in(arg_keys[18], 71), 0)
    stretch_v = bell_draw(arg_keys[3], (STRETCH, KV_HEADS * HEAD_DIM), 6.0, 36.0, ((0, 16), (1, 8)))
    prefix_k = draw_prefix_k(jax.random.fold_in(arg_keys[18], 71), 0)
    prefix_v = bell_draw(arg_keys[5], (PREFIX, KV_HEADS * HEAD_DIM), 6.0, 36.0, ((0, 16), (1, 8)))
    dec_len = draw_dec_len(jax.random.fold_in(arg_keys[18], 71), 0)
    dec_q = draw_dec_q(jax.random.fold_in(arg_keys[18], 71), 0)
    dec_k = bell_draw(arg_keys[8], (DROWS, KV_HEADS * HEAD_DIM), 1.0, 6.0, ((0, 16), (1, 8)))
    dec_v = bell_draw(arg_keys[9], (DROWS, KV_HEADS * HEAD_DIM), 6.0, 36.0, ((0, 16), (1, 8)))
    cache_k = draw_cache_k(jax.random.fold_in(arg_keys[18], 71), 0)
    cache_v = bell_draw(arg_keys[11], (DROWS, CACHE, KV_HEADS * HEAD_DIM), 6.0, 36.0, ((0, 16), (2, 8)))
    hand_owner_keys = jax.random.split(jax.random.fold_in(arg_keys[12], 1), NBLK // FIN_DEV)
    hand_owner_turns = jax.random.permutation(jax.random.fold_in(arg_keys[12], 3), NBLK // FIN_DEV)
    hand_owner = jax.vmap(lambda own, number: routed_block(jax.random.fold_in(arg_keys[12], 2), own, number, FIN_DEV, N_CTX, 1, MOST, 2))(hand_owner_keys, hand_owner_turns).reshape((NBLK, 1))
    hand_count = plant(jax.random.randint(arg_keys[13], (NBLK,), 1, BLK + 1), jax.random.fold_in(arg_keys[13], 1), 1, BLK).astype(jnp.int32)
    hand_q = draw_hand_q(jax.random.fold_in(arg_keys[18], 71), 0)
    hand_k = draw_hand_k(jax.random.fold_in(arg_keys[18], 71), 0)
    hand_v = bell_draw(arg_keys[16], (NBLK, BLK, KV_HEADS * HEAD_DIM), 6.0, 36.0, ((0, 16), (2, 8)))
    out_weight = bell_draw(arg_keys[17], (HEADS * HEAD_DIM, D), (HEADS * HEAD_DIM) ** -0.5, 0.0625, ((0, 8),))
    return dict(stretch_start=stretch_start, stretch_q=stretch_q, stretch_k=stretch_k, stretch_v=stretch_v, prefix_k=prefix_k, prefix_v=prefix_v, dec_len=dec_len, dec_q=dec_q, dec_k=dec_k, dec_v=dec_v, cache_k=cache_k, cache_v=cache_v, hand_owner=hand_owner, hand_count=hand_count, hand_q=hand_q, hand_k=hand_k, hand_v=hand_v, out_weight=out_weight)


NEG = -1e30


def soft_attend(queries, keys, values, valid):
    factor = HEAD_DIM ** -0.5
    scores = jnp.dot(queries, keys.T, preferred_element_type=jnp.float32) * factor
    scores = jnp.where(valid, scores, NEG)
    peak = jnp.max(scores, axis=-1, keepdims=True)
    expo = jnp.where(valid, jnp.exp(scores - peak), jnp.float32(0.0))
    total = jnp.sum(expo, axis=-1, keepdims=True)
    summed = jnp.dot(expo.astype(jnp.bfloat16), values, preferred_element_type=jnp.float32)
    return summed / jnp.where(total > 0, total, jnp.float32(1.0))


def grouped_attend(queries, keys, values, valid):
    return jax.vmap(soft_attend, in_axes=(0, 1, 1, None))(queries, keys, values, valid)


def reference(stretch_start, stretch_q, stretch_k, stretch_v, prefix_k, prefix_v, dec_len, dec_q, dec_k, dec_v, cache_k, cache_v, hand_owner, hand_count, hand_q, hand_k, hand_v, out_weight):
    group_size = HEADS // KV_HEADS
    key_rows = PREFIX + STRETCH
    all_keys = jnp.concatenate([prefix_k, stretch_k], 0).reshape(key_rows, KV_HEADS, HEAD_DIM).transpose(1, 0, 2)
    all_values = jnp.concatenate([prefix_v, stretch_v], 0).reshape(key_rows, KV_HEADS, HEAD_DIM).transpose(1, 0, 2)
    queries = stretch_q.reshape(STRETCH, HEADS, HEAD_DIM).transpose(1, 0, 2)
    token_pos = jnp.arange(STRETCH, dtype=jnp.int32)
    key_pos = jnp.arange(key_rows, dtype=jnp.int32)
    valid = jnp.where(key_pos[None, :] < PREFIX, (key_pos < stretch_start[0])[None, :], (key_pos[None, :] - PREFIX) <= token_pos[:, None])

    def one_head(head):
        return soft_attend(queries[head], all_keys[head // group_size], all_values[head // group_size], valid).astype(jnp.bfloat16)

    stretch_attn = lax.map(one_head, jnp.arange(HEADS, dtype=jnp.int32)).transpose(1, 0, 2).reshape(STRETCH, HEADS * HEAD_DIM)
    stretch_out = jnp.dot(stretch_attn, out_weight, preferred_element_type=jnp.float32).astype(jnp.bfloat16)

    slot_range = jnp.arange(CACHE + 1, dtype=jnp.int32)

    def one_row(row):
        keys = jnp.concatenate([cache_k[row], dec_k[row][None, :]], 0).reshape(CACHE + 1, KV_HEADS, HEAD_DIM)
        values = jnp.concatenate([cache_v[row], dec_v[row][None, :]], 0).reshape(CACHE + 1, KV_HEADS, HEAD_DIM)
        row_valid = ((slot_range < dec_len[row]) | (slot_range == CACHE))[None, :]
        row_query = dec_q[row].reshape(KV_HEADS, group_size, HEAD_DIM)
        return grouped_attend(row_query, keys, values, row_valid).reshape(HEADS * HEAD_DIM).astype(jnp.bfloat16)

    dec_attn = lax.map(one_row, jnp.arange(DROWS, dtype=jnp.int32))
    dec_out = jnp.dot(dec_attn, out_weight, preferred_element_type=jnp.float32).astype(jnp.bfloat16)

    owners = hand_owner[:, 0].reshape(N_CTX, FIN_DEV)
    same_owner = owners[:, :, None] == owners[:, None, :]
    block_range = jnp.arange(FIN_DEV, dtype=jnp.int32)
    earlier = block_range[None, :] < block_range[:, None]
    ranking = jnp.sum((same_owner & earlier[None, :, :]).astype(jnp.int32), axis=-1)
    slot_index = (owners * SLOTS + jnp.arange(N_CTX, dtype=jnp.int32)[:, None] * MOST + ranking).reshape(NBLK)
    block_range_full = jnp.arange(BLK, dtype=jnp.int32)

    def one_block(block):
        keys = hand_k[block].reshape(BLK, KV_HEADS, HEAD_DIM)
        values = hand_v[block].reshape(BLK, KV_HEADS, HEAD_DIM)
        block_valid = (block_range_full < hand_count[block])[None, :]
        block_query = hand_q[block].reshape(KV_HEADS, group_size, HEAD_DIM)
        return grouped_attend(block_query, keys, values, block_valid).reshape(HEADS * HEAD_DIM).astype(jnp.bfloat16)

    block_attn = lax.map(one_block, jnp.arange(NBLK, dtype=jnp.int32))
    block_out = jnp.dot(block_attn, out_weight, preferred_element_type=jnp.float32).astype(jnp.bfloat16)
    new_out = jnp.zeros((NEW_ROWS, D), jnp.bfloat16).at[slot_index].set(block_out)
    return stretch_out, dec_out, new_out
```

```python
import functools
import math

import jax
import jax.numpy as jnp
from jax import lax
from jax.experimental import pallas as pl
from jax.experimental.pallas import tpu as pltpu
from jax.sharding import PartitionSpec as P

HEAD_DIM = 128
MOST = 2
GROUP = 8
TOK = 128
PRE = 1024
BLOCK = PRE + TOK
ROWS = GROUP * TOK
TILE = 512
SUB = 256
NEG = -1e30
SCALE = math.log2(math.e) / math.sqrt(HEAD_DIM)
LOW, HIGH = 2.0**-60, 2.0**100
VMEM_LIMIT = 24 * 2**20
STATS = 32


def dot_t(a, b):
    return lax.dot_general(a, b, (((1,), (1,)), ((), ())), preferred_element_type=jnp.float32)


def dot(a, b):
    return jnp.dot(a, b, preferred_element_type=jnp.float32)


def ctx_index(y, x, c):
    return y * 8 + x * 2 + c


def ctx_perm(move):
    return [
        (ctx_index(y, x, c), ctx_index(*move(y, x, c)))
        for y in range(2)
        for x in range(4)
        for c in range(2)
    ]


X_UP = ctx_perm(lambda y, x, c: (y, (x + 1) % 4, c))
X_DOWN = ctx_perm(lambda y, x, c: (y, (x + 3) % 4, c))
X_TWO = ctx_perm(lambda y, x, c: (y, (x + 2) % 4, c))
Y_SWAP = ctx_perm(lambda y, x, c: (1 - y, x, c))
CORE_SWAP = ctx_perm(lambda y, x, c: (y, x, 1 - c))


def lane_sums(p):
    total = p[:, 0:128]
    for at in range(128, p.shape[1], 128):
        total = total + p[:, at : at + 128]
    return total


def stack_queries(q_refs, queries):
    for half, ref in enumerate(q_refs):
        for head in range(GROUP):
            queries[pl.ds(half * ROWS + head * TOK, TOK), :] = ref[:, pl.ds(head * HEAD_DIM, HEAD_DIM)]


def add_block(info, block_at, kv, queries, acc, sums, halves):
    prefix_end = info[0]
    chunk = info[3 + block_at]
    count = jnp.clip(prefix_end - chunk * PRE, 0, PRE)

    @pl.when(count == PRE)
    def _():
        for tile in range(len(halves) * ROWS // TILE):
            rows = pl.ds(tile * TILE, TILE)
            for at in range(0, PRE, 512):
                p = jnp.exp2(dot_t(queries[rows, :], kv[pl.ds(at, 512), :]) * SCALE)
                acc[rows, :] += dot(p.astype(jnp.bfloat16), kv[pl.ds(BLOCK + at, 512), :])
                sums[rows, :] += lane_sums(p)

    @pl.when(jnp.logical_and(count > 0, count < PRE))
    def _():
        def step(at, carry):
            start = pl.multiple_of(at * SUB, SUB)
            columns = start + lax.broadcasted_iota(jnp.int32, (TILE, SUB), 1)
            for tile in range(len(halves) * ROWS // TILE):
                rows = pl.ds(tile * TILE, TILE)
                s = dot_t(queries[rows, :], kv[pl.ds(start, SUB), :]) * SCALE
                p = jnp.where(columns < count, jnp.exp2(s), 0.0)
                acc[rows, :] += dot(p.astype(jnp.bfloat16), kv[pl.ds(BLOCK + start, SUB), :])
                sums[rows, :] += lane_sums(p)
            return carry

        lax.fori_loop(0, (count + SUB - 1) // SUB, step, 0)

    for at_half, half in enumerate(halves):
        place = info[1 + half]

        @pl.when(chunk <= place)
        def _():
            token = lax.broadcasted_iota(jnp.int32, (TILE, TOK), 0) % TOK
            key = lax.broadcasted_iota(jnp.int32, (TILE, TOK), 1)
            seen = key <= token + jnp.where(chunk < place, TOK, 0)
            for tile in range(ROWS // TILE):
                rows = pl.ds(at_half * ROWS + tile * TILE, TILE)
                s = dot_t(queries[rows, :], kv[pl.ds(PRE, TOK), :]) * SCALE
                p = jnp.where(seen, jnp.exp2(s), 0.0)
                acc[rows, :] += dot(p.astype(jnp.bfloat16), kv[pl.ds(BLOCK + PRE, TOK), :])
                sums[rows, :] += p


def shifted_step(rows, s, seen, values, queries, acc, sums, peak):
    s = jnp.where(seen, s, NEG)
    before = peak[rows, :]
    now = jnp.maximum(before, jnp.max(s, axis=1, keepdims=True))
    p = jnp.where(seen, jnp.exp2(s - now[:, 0:1]), 0.0)
    fade = jnp.exp2(before - now)
    acc[rows, :] = acc[rows, :] * fade + dot(p.astype(jnp.bfloat16), values)
    sums[rows, :] = sums[rows, :] * fade + lane_sums(p)
    peak[rows, :] = now


def shifted_block(info, chunk, place, kv, queries, acc, sums, peak):
    count = jnp.clip(info[0] - chunk * PRE, 0, PRE)
    tile_rows = 256

    def tile_step(tile, carry):
        rows = pl.ds(pl.multiple_of(tile * tile_rows, tile_rows), tile_rows)

        def step(at, carry):
            start = pl.multiple_of(at * SUB, SUB)
            columns = start + lax.broadcasted_iota(jnp.int32, (tile_rows, SUB), 1)
            s = dot_t(queries[rows, :], kv[pl.ds(start, SUB), :]) * SCALE
            shifted_step(rows, s, columns < count, kv[pl.ds(BLOCK + start, SUB), :], queries, acc, sums, peak)
            return carry

        lax.fori_loop(0, (count + SUB - 1) // SUB, step, 0)

        @pl.when(chunk <= place)
        def _():
            token = lax.broadcasted_iota(jnp.int32, (tile_rows, TOK), 0) % TOK
            key = lax.broadcasted_iota(jnp.int32, (tile_rows, TOK), 1)
            seen = key <= token + jnp.where(chunk < place, TOK, 0)
            s = dot_t(queries[rows, :], kv[pl.ds(PRE, TOK), :]) * SCALE
            shifted_step(rows, s, seen, kv[pl.ds(BLOCK + PRE, TOK), :], queries, acc, sums, peak)

        return carry

    lax.fori_loop(0, ROWS // tile_rows, tile_step, 0)


def attend_kernel(first_block, blocks, starts, info, own_ref, other_ref, *refs):
    kvs, refs = refs[:blocks], refs[blocks:]
    if not starts:
        (acc_in, sums_in), refs = refs[:2], refs[2:]
    acc, sums, queries = refs
    stack_queries((own_ref, other_ref), queries)
    if starts:
        acc[...] = jnp.zeros_like(acc)
        sums[...] = jnp.zeros_like(sums)
    else:
        acc[...] = acc_in[...]
        sums[...] = sums_in[...]
    for at in range(blocks):
        add_block(info, first_block + at, kvs[at], queries, acc, sums, (0, 1))


def last_kernel(half, earlier, blocks, info, q_ref, *refs):
    earlier_kvs, refs = refs[:earlier], refs[earlier:]
    kvs, refs = refs[:blocks], refs[blocks:]
    acc_in, sums_in, out, queries, acc, sums, peak, held, levels, sem = refs
    stack_queries((q_ref,), queries)
    acc[...] = acc_in[...]
    sums[...] = sums_in[...]
    for at in range(blocks):
        add_block(info, earlier + at, kvs[at], queries, acc, sums, (half,))
    peak[...] = jnp.zeros_like(peak)
    has_keys = jnp.int32(0)
    for at in range(earlier + blocks):
        chunk = info[3 + at]
        some = jnp.logical_or(info[0] > chunk * PRE, chunk <= info[1 + half])
        has_keys = jnp.where(some, 1, has_keys)
    total = jnp.sum(sums[...], axis=1, keepdims=True)
    inside = jnp.where(jnp.logical_and(total >= LOW, total <= HIGH), 1.0, 0.0)

    @pl.when(jnp.logical_and(has_keys > 0, jnp.min(inside) < 0.5))
    def _():
        acc[...] = jnp.zeros_like(acc)
        sums[...] = jnp.zeros_like(sums)
        peak[...] = jnp.full_like(peak, NEG)

        def block_step(at, carry):
            for one in range(earlier + blocks):
                source = earlier_kvs[one] if one < earlier else kvs[one - earlier]

                @pl.when(at == one)
                def _():
                    copy = pltpu.make_async_copy(source, held, sem)
                    copy.start()
                    copy.wait()

            shifted_block(info, info[3 + at], info[1 + half], held, queries, acc, sums, peak)
            return carry

        lax.fori_loop(0, earlier + blocks, block_step, 0)

    for head in range(GROUP):
        rows = pl.ds(head * TOK, TOK)
        total = jnp.sum(sums[rows, :], axis=1, keepdims=True)
        out[rows, :] = (acc[rows, :] / jnp.where(total > 0, total, 1.0)).astype(out.dtype)
        level = jnp.where(total > 0, peak[rows, :] + jnp.log2(jnp.where(total > 0, total, 1.0)), NEG)
        levels[pl.ds(head, 1), :] = jnp.transpose(level)[0:1, :]
    high = levels[...].astype(jnp.bfloat16)
    rest = levels[...] - high.astype(jnp.float32)
    middle = rest.astype(jnp.bfloat16)
    low = (rest - middle.astype(jnp.float32)).astype(jnp.bfloat16)
    out[pl.ds(ROWS, STATS), :] = jnp.concatenate([high, middle, low, jnp.zeros_like(low)], 0)


def unpack_levels(packed):
    pieces = [packed[pl.ds(ROWS, STATS), :].astype(jnp.float32)]
    return pieces[0][0:8] + pieces[0][8:16] + pieces[0][16:24]


def whole(shape):
    return pl.BlockSpec(shape, lambda *_: (0,) * len(shape))


SMEM = pl.BlockSpec(memory_space=pltpu.SMEM)
STATE = jax.ShapeDtypeStruct((2 * ROWS, 128), jnp.float32)


def attend_cost(blocks):
    return pl.CostEstimate(
        flops=blocks * 4 * 2 * ROWS * BLOCK * HEAD_DIM * 2,
        bytes_accessed=blocks * BLOCK * 512 + 4 * 2 * ROWS * 512,
        transcendentals=blocks * 2 * ROWS * BLOCK,
    )


def attend(info, own_q, other_q, first_block, kvs, state, name):
    blocks = len(kvs)
    state = state or ()
    return pl.pallas_call(
        functools.partial(attend_kernel, first_block, blocks, not state),
        out_shape=(STATE, STATE),
        in_specs=[SMEM] + [whole(own_q.shape)] * 2 + [whole(kv.shape) for kv in kvs] + [whole(STATE.shape)] * len(state),
        out_specs=(whole(STATE.shape),) * 2,
        scratch_shapes=[pltpu.VMEM((2 * ROWS, HEAD_DIM), jnp.bfloat16)],
        compiler_params=pltpu.CompilerParams(vmem_limit_bytes=VMEM_LIMIT),
        cost_estimate=attend_cost(blocks),
        name=name,
    )(info, own_q, other_q, *kvs, *state)


def attend_last(info, q, half, earlier, kvs, state, name):
    blocks = len(kvs)
    packed = jax.ShapeDtypeStruct((ROWS + STATS, HEAD_DIM), jnp.bfloat16)
    rows = pl.BlockSpec((ROWS, 128), lambda *_: (half, 0))
    return pl.pallas_call(
        functools.partial(last_kernel, half, len(earlier), blocks),
        grid=(1,),
        out_shape=packed,
        in_specs=[SMEM, whole(q.shape)]
        + [pl.BlockSpec(memory_space=pl.ANY)] * len(earlier)
        + [whole(kv.shape) for kv in kvs]
        + [rows] * 2,
        out_specs=whole(packed.shape),
        scratch_shapes=[
            pltpu.VMEM((ROWS, HEAD_DIM), jnp.bfloat16),
            pltpu.VMEM((ROWS, 128), jnp.float32),
            pltpu.VMEM((ROWS, 128), jnp.float32),
            pltpu.VMEM((ROWS, 128), jnp.float32),
            pltpu.VMEM((2 * BLOCK, HEAD_DIM), jnp.bfloat16),
            pltpu.VMEM((GROUP, TOK), jnp.float32),
            pltpu.SemaphoreType.DMA(()),
        ],
        compiler_params=pltpu.CompilerParams(vmem_limit_bytes=VMEM_LIMIT),
        cost_estimate=attend_cost(blocks),
        name=name,
    )(info, q, *earlier, *kvs, *state)


def softmax_rows(s, seen):
    s = jnp.where(seen, s, NEG)
    return s, jnp.max(s, axis=1, keepdims=True)


def spread(rows, flat):
    for head in range(GROUP):
        piece = rows[:, pl.ds(head * HEAD_DIM, HEAD_DIM)].astype(jnp.float32)
        flat[pl.ds(head, rows.shape[0], stride=GROUP), :] = piece


def gather_heads(flat, rows):
    for head in range(GROUP):
        piece = flat[pl.ds(head, rows.shape[0], stride=GROUP), :]
        rows[:, pl.ds(head * HEAD_DIM, HEAD_DIM)] = piece.astype(rows.dtype)


def heads_at(row):
    return pl.ds(pl.multiple_of(row * GROUP, GROUP), GROUP)


def rows_kernel(
    dec_len, owner, hand_count, dec_q, dec_k, dec_v, hand_q, cache_k, cache_v, hand_k, hand_v, dec_out, slot_out,
    dec_rows, hand_rows, keys, values, dec_sums, slot_sums, taken,
):
    row = pl.program_id(0)
    per = hand_k.shape[0]

    @pl.when(row == 0)
    def _():
        count = dec_q.shape[0]
        spread(dec_q, dec_rows)
        spread(hand_q, hand_rows)
        keys[pl.ds(0, count), :] = dec_k[...].astype(jnp.float32)
        values[pl.ds(0, count), :] = dec_v[...].astype(jnp.float32)
        dec_sums[...] = jnp.zeros_like(dec_sums)
        slot_sums[...] = jnp.zeros_like(slot_sums)
        for at in range(taken.shape[0]):
            taken[at] = 0

    q = dec_rows[heads_at(row), :].astype(jnp.bfloat16)
    s = dot_t(q, cache_k[0]) * SCALE
    seen = lax.broadcasted_iota(jnp.int32, s.shape, 1) < dec_len[row]
    s, top = softmax_rows(s, seen)
    own = jnp.sum(q.astype(jnp.float32) * keys[pl.ds(row, 1), :], axis=1, keepdims=True) * SCALE
    top = jnp.maximum(top, own)
    p = jnp.where(seen, jnp.exp2(s - top), 0.0)
    own = jnp.exp2(own - top)
    total = jnp.sum(p, axis=1, keepdims=True) + own
    summed = dot(p.astype(jnp.bfloat16), cache_v[0])
    summed = summed + own.astype(jnp.bfloat16).astype(jnp.float32) * values[pl.ds(row, 1), :]
    dec_sums[heads_at(row), :] = summed / total
    for one in range(per):
        at = row * per + one
        s = dot_t(hand_rows[heads_at(at), :].astype(jnp.bfloat16), hand_k[one]) * SCALE
        seen = lax.broadcasted_iota(jnp.int32, s.shape, 1) < hand_count[at]
        s, top = softmax_rows(s, seen)
        p = jnp.where(seen, jnp.exp2(s - top), 0.0)
        total = jnp.sum(p, axis=1, keepdims=True)
        summed = dot(p.astype(jnp.bfloat16), hand_v[one])
        to = owner[at]
        slot_sums[heads_at(to * MOST + taken[to]), :] = summed / jnp.where(total > 0, total, 1.0)
        taken[to] = taken[to] + 1

    @pl.when(row == pl.num_programs(0) - 1)
    def _():
        gather_heads(dec_sums, dec_out)
        gather_heads(slot_sums, slot_out)


def attend_rows(dec_len, owner, hand_count, dec_q, dec_k, dec_v, hand_q, cache_k, cache_v, hand_k, hand_v, owners):
    rows, slots = cache_k.shape[:2]
    blocks, depth = hand_k.shape[:2]
    per = blocks // rows
    width = dec_q.shape[1]

    def spec(count, *shape):
        return pl.BlockSpec((count, *shape), lambda i: (i,) + (0,) * len(shape))

    return pl.pallas_call(
        rows_kernel,
        grid=(rows,),
        out_shape=(
            jax.ShapeDtypeStruct((16, width), jnp.bfloat16),
            jax.ShapeDtypeStruct((owners * MOST, width), jnp.bfloat16),
        ),
        in_specs=[SMEM] * 3
        + [whole(a.shape) for a in (dec_q, dec_k, dec_v, hand_q)]
        + [
            spec(1, slots, HEAD_DIM),
            spec(1, slots, HEAD_DIM),
            spec(per, depth, HEAD_DIM),
            spec(per, depth, HEAD_DIM),
        ],
        out_specs=(whole((16, width)), whole((owners * MOST, width))),
        scratch_shapes=[
            pltpu.VMEM((rows * GROUP, HEAD_DIM), jnp.float32),
            pltpu.VMEM((blocks * GROUP, HEAD_DIM), jnp.float32),
            pltpu.VMEM((8, HEAD_DIM), jnp.float32),
            pltpu.VMEM((8, HEAD_DIM), jnp.float32),
            pltpu.VMEM((16 * GROUP, HEAD_DIM), jnp.float32),
            pltpu.VMEM((owners * MOST * GROUP, HEAD_DIM), jnp.float32),
            pltpu.SMEM((owners,), jnp.int32),
        ],
        compiler_params=pltpu.CompilerParams(vmem_limit_bytes=56 * 2**20),
        cost_estimate=pl.CostEstimate(flops=10**9, bytes_accessed=6 * 2**20, transcendentals=10**5),
        name="rows",
    )(dec_len, owner, hand_count, dec_q, dec_k, dec_v, hand_q, cache_k, cache_v, hand_k, hand_v)


def join_kernel(*refs):
    sources, out, sems = refs[:4], refs[4], refs[5]
    copies = []
    at = 0
    for n, source in enumerate(sources):
        copies.append(pltpu.make_async_copy(source, out.at[pl.ds(at, source.shape[0])], sems.at[n]))
        at += source.shape[0]
    for copy in copies:
        copy.start()
    for copy in copies:
        copy.wait()


def join(*pieces):
    rows = sum(piece.shape[0] for piece in pieces)
    return pl.pallas_call(
        join_kernel,
        out_shape=jax.ShapeDtypeStruct((rows, HEAD_DIM), jnp.bfloat16),
        in_specs=[pl.BlockSpec(memory_space=pl.ANY)] * 4,
        out_specs=whole((rows, HEAD_DIM)),
        scratch_shapes=[pltpu.SemaphoreType.DMA((4,))],
        compiler_params=pltpu.CompilerParams(vmem_limit_bytes=8 * 2**20),
        cost_estimate=pl.CostEstimate(flops=0, bytes_accessed=rows * 512, transcendentals=0),
        name="join",
    )(*pieces)


def column(row):
    return jnp.transpose(jnp.broadcast_to(row, (TOK, TOK)))


def project_kernel(parts, me, mine, other, new, dec, weight, *refs):
    outs, attn = refs[:parts], refs[parts]
    step = pl.program_id(0)

    @pl.when(step == 0)
    def _():
        a_levels, b_levels = unpack_levels(mine), unpack_levels(other)
        top = jnp.maximum(a_levels, b_levels)
        wa, wb = jnp.exp2(a_levels - top), jnp.exp2(b_levels - top)
        wa, wb = wa / (wa + wb), wb / (wa + wb)
        for head in range(GROUP):
            rows = pl.ds(head * TOK, TOK)
            a, b = mine[rows, :].astype(jnp.float32), other[rows, :].astype(jnp.float32)
            mixed = a * column(wa[head : head + 1, :]) + b * column(wb[head : head + 1, :])
            attn[pl.ds(0, TOK), pl.ds(head * HEAD_DIM, HEAD_DIM)] = mixed.astype(attn.dtype)
        attn[pl.ds(TOK, new.shape[0]), :] = new[...]
        attn[pl.ds(TOK + new.shape[0], dec.shape[0]), :] = dec[...]

    result = dot(attn[...], weight[...]).astype(jnp.bfloat16)
    for part in range(parts):

        @pl.when(step == part)
        def _():
            outs[part][...] = result[: outs[part].shape[0]]


def project(me, mine, other, new, dec, weight, rows, parts):
    depth, width = weight.shape
    columns = width // parts
    out = jax.ShapeDtypeStruct((rows, columns), jnp.bfloat16)
    return pl.pallas_call(
        functools.partial(project_kernel, parts),
        grid_spec=pltpu.PrefetchScalarGridSpec(
            num_scalar_prefetch=1,
            grid=(parts,),
            in_specs=[
                whole(mine.shape),
                whole(other.shape),
                whole(new.shape),
                whole(dec.shape),
                pl.BlockSpec((depth, columns), lambda i, me: (0, me[0] ^ i)),
            ],
            out_specs=[whole(out.shape)] * parts,
            scratch_shapes=[pltpu.VMEM((TOK + new.shape[0] + dec.shape[0], depth), jnp.bfloat16)],
        ),
        out_shape=[out] * parts,
        compiler_params=pltpu.CompilerParams(vmem_limit_bytes=VMEM_LIMIT),
        cost_estimate=pl.CostEstimate(flops=2 * TOK * depth * width, bytes_accessed=2 * depth * width, transcendentals=0),
        name="project",
    )(me, mine, other, new, dec, weight)


def total_kernel(*refs):
    parts, outs = refs[:-3], refs[-3:]
    total = parts[0][...].astype(jnp.float32)
    for part in parts[1:]:
        total = total + part[...].astype(jnp.float32)
    total = total.astype(jnp.bfloat16)
    at = 0
    for out in outs:
        out[...] = total[at : at + out.shape[0]]
        at += out.shape[0]


def add_up(parts, rows):
    width = parts[0].shape[1]
    return pl.pallas_call(
        total_kernel,
        out_shape=[jax.ShapeDtypeStruct((count, width), jnp.bfloat16) for count in rows],
        in_specs=[whole(part.shape) for part in parts],
        out_specs=[whole((count, width)) for count in rows],
        compiler_params=pltpu.CompilerParams(vmem_limit_bytes=VMEM_LIMIT),
        cost_estimate=pl.CostEstimate(flops=0, bytes_accessed=len(parts) * sum(rows) * width * 2, transcendentals=0),
        name="add_up",
    )(*parts)


def local(
    stretch_start,
    stretch_q,
    stretch_k,
    stretch_v,
    prefix_k,
    prefix_v,
    dec_len,
    dec_q,
    dec_k,
    dec_v,
    cache_k,
    cache_v,
    hand_owner,
    hand_count,
    hand_q,
    hand_k,
    hand_v,
    out_weight,
):
    place = lax.axis_index("ctx")
    me = lax.axis_index("tp")
    parts = lax.axis_size("tp")
    y, x, c = place // 8, (place // 2) % 4, place % 2

    b0 = join(prefix_k, stretch_k, prefix_v, stretch_v)
    b1 = lax.ppermute(b0, "ctx", X_UP)
    b2 = lax.ppermute(b0, "ctx", X_DOWN)
    c0 = lax.ppermute(b0, "ctx", CORE_SWAP)
    other_q = lax.ppermute(stretch_q, "ctx", Y_SWAP)
    up, down, two = (x + 1) % 4, (x + 3) % 4, (x + 2) % 4
    info = jnp.stack(
        [
            stretch_start[0],
            place,
            ctx_index(1 - y, x, c),
            place,
            ctx_index(y, x, 1 - c),
            ctx_index(y, down, c),
            ctx_index(y, down, 1 - c),
            ctx_index(y, up, c),
            ctx_index(y, up, 1 - c),
            ctx_index(y, two, c),
            ctx_index(y, two, 1 - c),
        ]
    ).astype(jnp.int32)

    ctx_count = lax.axis_size("ctx")
    dec_attn, slot_attn = attend_rows(
        dec_len, hand_owner[:, 0], hand_count, dec_q, dec_k, dec_v, hand_q, cache_k, cache_v, hand_k, hand_v, ctx_count
    )
    new_attn = lax.all_to_all(slot_attn, "ctx", split_axis=0, concat_axis=0, tiled=True)
    info, b0_later, _ = lax.optimization_barrier((info, b0, dec_attn))
    b4 = lax.ppermute(b0_later, "ctx", X_TWO)

    state = attend(info, stretch_q, other_q, 0, [b0, c0], None, "attend_a")
    c1 = lax.ppermute(b1, "ctx", CORE_SWAP)
    c2 = lax.ppermute(b2, "ctx", CORE_SWAP)
    state = attend(info, stretch_q, other_q, 2, [b1, c1, b2, c2], state, "attend_b")
    c4 = lax.ppermute(b4, "ctx", CORE_SWAP)
    before = [b0, c0, b1, c1, b2, c2]
    give = attend_last(info, other_q, 1, before, [b4, c4], state, "attend_give")
    other = lax.ppermute(give, "ctx", Y_SWAP)
    mine = attend_last(info, stretch_q, 0, before, [b4, c4], state, "attend_keep")

    counts = (TOK, new_attn.shape[0], dec_q.shape[0])
    sent = project(me[None].astype(jnp.int32), mine, other, new_attn, dec_attn, out_weight, sum(counts), parts)
    got = [sent[0]] + [
        lax.ppermute(sent[k], "tp", [(i, i ^ k) for i in range(parts)]) for k in range(1, parts)
    ]
    stretch_out, new_out, dec_out = add_up(got, counts)
    return stretch_out, dec_out, new_out


def solution(mesh):
    in_specs = (
        P(),
        P("ctx", "tp"),
        P("ctx", "tp"),
        P("ctx", "tp"),
        P("ctx", "tp"),
        P("ctx", "tp"),
        P("ctx"),
        P("ctx", "tp"),
        P("ctx", "tp"),
        P("ctx", "tp"),
        P("ctx", None, "tp"),
        P("ctx", None, "tp"),
        P("ctx", None),
        P("ctx"),
        P("ctx", "tp"),
        P("ctx", None, "tp"),
        P("ctx", None, "tp"),
        P("tp", None),
    )
    out_specs = (P("ctx", "tp"), P("ctx", "tp"), P("ctx", "tp"))
    return jax.shard_map(local, mesh=mesh, in_specs=in_specs, out_specs=out_specs, check_vma=False)
```

```python
import functools
import math

import jax
import jax.numpy as jnp
from jax import lax
from jax.experimental import pallas as pl
from jax.experimental.pallas import tpu as pltpu
from jax.sharding import PartitionSpec as P

HEAD_DIM = 128
MOST = 2
GROUP = 8
TOK = 128
PRE = 1024
BLOCK = PRE + TOK
ROWS = GROUP * TOK
TILE = 512
SUB = 256
NEG = -1e30
SCALE = math.log2(math.e) / math.sqrt(HEAD_DIM)
LOW, HIGH = 2.0**-60, 2.0**100
VMEM_LIMIT = 24 * 2**20
STATS = 32


def dot_t(a, b):
    return lax.dot_general(a, b, (((1,), (1,)), ((), ())), preferred_element_type=jnp.float32)


def dot(a, b):
    return jnp.dot(a, b, preferred_element_type=jnp.float32)


def ctx_index(y, x, c):
    return y * 8 + x * 2 + c


def ctx_perm(move):
    return [
        (ctx_index(y, x, c), ctx_index(*move(y, x, c)))
        for y in range(2)
        for x in range(4)
        for c in range(2)
    ]


X_UP = ctx_perm(lambda y, x, c: (y, (x + 1) % 4, c))
X_DOWN = ctx_perm(lambda y, x, c: (y, (x + 3) % 4, c))
X_TWO = ctx_perm(lambda y, x, c: (y, (x + 2) % 4, c))
Y_SWAP = ctx_perm(lambda y, x, c: (1 - y, x, c))
CORE_SWAP = ctx_perm(lambda y, x, c: (y, x, 1 - c))


def tp_index(h, z):
    return h * 4 + z % 4


def tp_perm(move):
    return [(tp_index(h, z), tp_index(*move(h, z))) for h in range(2) for z in range(4)]


Z_UP = tp_perm(lambda h, z: (h, z + 1))
Z_DOWN = tp_perm(lambda h, z: (h, z + 3))
Z_TWO = tp_perm(lambda h, z: (h, z + 2))
H_SWAP = tp_perm(lambda h, z: (1 - h, z))


def lane_sums(p):
    total = p[:, 0:128]
    for at in range(128, p.shape[1], 128):
        total = total + p[:, at : at + 128]
    return total


def stack_queries(q_refs, queries):
    for half, ref in enumerate(q_refs):
        for head in range(GROUP):
            queries[pl.ds(half * ROWS + head * TOK, TOK), :] = ref[:, pl.ds(head * HEAD_DIM, HEAD_DIM)]


def add_block(info, block_at, kv, queries, acc, sums, halves):
    prefix_end = info[0]
    chunk = info[3 + block_at]
    count = jnp.clip(prefix_end - chunk * PRE, 0, PRE)

    @pl.when(count == PRE)
    def _():
        for tile in range(len(halves) * ROWS // TILE):
            rows = pl.ds(tile * TILE, TILE)
            for at in range(0, PRE, 512):
                p = jnp.exp2(dot_t(queries[rows, :], kv[pl.ds(at, 512), :]) * SCALE)
                acc[rows, :] += dot(p.astype(jnp.bfloat16), kv[pl.ds(BLOCK + at, 512), :])
                sums[rows, :] += lane_sums(p)

    @pl.when(jnp.logical_and(count > 0, count < PRE))
    def _():
        def step(at, carry):
            start = pl.multiple_of(at * SUB, SUB)
            columns = start + lax.broadcasted_iota(jnp.int32, (TILE, SUB), 1)
            for tile in range(len(halves) * ROWS // TILE):
                rows = pl.ds(tile * TILE, TILE)
                s = dot_t(queries[rows, :], kv[pl.ds(start, SUB), :]) * SCALE
                p = jnp.where(columns < count, jnp.exp2(s), 0.0)
                acc[rows, :] += dot(p.astype(jnp.bfloat16), kv[pl.ds(BLOCK + start, SUB), :])
                sums[rows, :] += lane_sums(p)
            return carry

        lax.fori_loop(0, (count + SUB - 1) // SUB, step, 0)


def add_tokens(info, first_block, kvs, queries, acc, sums, halves, near):
    count = len(kvs)
    width = count * TOK
    for at, kv in enumerate(kvs):
        near[pl.ds(at * TOK, TOK), :] = kv[pl.ds(PRE, TOK), :]
        near[pl.ds(width + at * TOK, TOK), :] = kv[pl.ds(BLOCK + PRE, TOK), :]
    for at_half, half in enumerate(halves):
        place = info[1 + half]
        seen_from = [place - info[3 + first_block + at] for at in range(count)]
        some = functools.reduce(jnp.maximum, seen_from)

        @pl.when(some >= 0)
        def _():
            column = lax.broadcasted_iota(jnp.int32, (1, width), 1)
            start = jnp.zeros((1, width), jnp.int32)
            for at in range(count):
                least = jnp.where(seen_from[at] > 0, -TOK, jnp.where(seen_from[at] == 0, 0, TOK))
                start = jnp.where(column // TOK == at, least, start)
            start = start + column % TOK
            token = lax.broadcasted_iota(jnp.int32, (TILE, width), 0) % TOK
            seen = start <= token
            for tile in range(ROWS // TILE):
                rows = pl.ds(at_half * ROWS + tile * TILE, TILE)
                s = dot_t(queries[rows, :], near[pl.ds(0, width), :]) * SCALE
                p = jnp.where(seen, jnp.exp2(s), 0.0)
                acc[rows, :] += dot(p.astype(jnp.bfloat16), near[pl.ds(width, width), :])
                sums[rows, :] += lane_sums(p)


def shifted_step(rows, s, seen, values, queries, acc, sums, peak):
    s = jnp.where(seen, s, NEG)
    before = peak[rows, :]
    now = jnp.maximum(before, jnp.max(s, axis=1, keepdims=True))
    p = jnp.where(seen, jnp.exp2(s - now[:, 0:1]), 0.0)
    fade = jnp.exp2(before - now)
    acc[rows, :] = acc[rows, :] * fade + dot(p.astype(jnp.bfloat16), values)
    sums[rows, :] = sums[rows, :] * fade + lane_sums(p)
    peak[rows, :] = now


def shifted_block(info, chunk, place, kv, queries, acc, sums, peak):
    count = jnp.clip(info[0] - chunk * PRE, 0, PRE)
    tile_rows = 256

    def tile_step(tile, carry):
        rows = pl.ds(pl.multiple_of(tile * tile_rows, tile_rows), tile_rows)

        def step(at, carry):
            start = pl.multiple_of(at * SUB, SUB)
            columns = start + lax.broadcasted_iota(jnp.int32, (tile_rows, SUB), 1)
            s = dot_t(queries[rows, :], kv[pl.ds(start, SUB), :]) * SCALE
            shifted_step(rows, s, columns < count, kv[pl.ds(BLOCK + start, SUB), :], queries, acc, sums, peak)
            return carry

        lax.fori_loop(0, (count + SUB - 1) // SUB, step, 0)

        @pl.when(chunk <= place)
        def _():
            token = lax.broadcasted_iota(jnp.int32, (tile_rows, TOK), 0) % TOK
            key = lax.broadcasted_iota(jnp.int32, (tile_rows, TOK), 1)
            seen = key <= token + jnp.where(chunk < place, TOK, 0)
            s = dot_t(queries[rows, :], kv[pl.ds(PRE, TOK), :]) * SCALE
            shifted_step(rows, s, seen, kv[pl.ds(BLOCK + PRE, TOK), :], queries, acc, sums, peak)

        return carry

    lax.fori_loop(0, ROWS // tile_rows, tile_step, 0)


def attend_kernel(halves, first_block, blocks, starts, info, *refs):
    count = len(halves)
    q_refs, refs = refs[:count], refs[count:]
    kvs, refs = refs[:blocks], refs[blocks:]
    if not starts:
        before, refs = refs[: 2 * count], refs[2 * count :]
    after, (queries, acc, sums, near) = refs[: 2 * count], refs[2 * count :]
    stack_queries(q_refs, queries)
    if starts:
        acc[...] = jnp.zeros_like(acc)
        sums[...] = jnp.zeros_like(sums)
    else:
        for at in range(count):
            acc[pl.ds(at * ROWS, ROWS), :] = before[2 * at][...]
            sums[pl.ds(at * ROWS, ROWS), :] = before[2 * at + 1][...]
    for at in range(blocks):
        add_block(info, first_block + at, kvs[at], queries, acc, sums, halves)
    add_tokens(info, first_block, kvs, queries, acc, sums, halves, near)
    for at in range(count):
        after[2 * at][...] = acc[pl.ds(at * ROWS, ROWS), :]
        after[2 * at + 1][...] = sums[pl.ds(at * ROWS, ROWS), :]


def last_kernel(half, earlier, blocks, info, q_ref, *refs):
    earlier_kvs, refs = refs[:earlier], refs[earlier:]
    kvs, refs = refs[:blocks], refs[blocks:]
    acc_in, sums_in, out, queries, acc, sums, near, peak, held, levels, sem = refs
    stack_queries((q_ref,), queries)
    acc[...] = acc_in[...]
    sums[...] = sums_in[...]
    for at in range(blocks):
        add_block(info, earlier + at, kvs[at], queries, acc, sums, (half,))
    add_tokens(info, earlier, kvs, queries, acc, sums, (half,), near)
    peak[...] = jnp.zeros_like(peak)
    has_keys = jnp.int32(0)
    for at in range(earlier + blocks):
        chunk = info[3 + at]
        some = jnp.logical_or(info[0] > chunk * PRE, chunk <= info[1 + half])
        has_keys = jnp.where(some, 1, has_keys)
    total = jnp.sum(sums[...], axis=1, keepdims=True)
    inside = jnp.where(jnp.logical_and(total >= LOW, total <= HIGH), 1.0, 0.0)

    @pl.when(jnp.logical_and(has_keys > 0, jnp.min(inside) < 0.5))
    def _():
        acc[...] = jnp.zeros_like(acc)
        sums[...] = jnp.zeros_like(sums)
        peak[...] = jnp.full_like(peak, NEG)

        def block_step(at, carry):
            for one in range(earlier + blocks):
                source = earlier_kvs[one] if one < earlier else kvs[one - earlier]

                @pl.when(at == one)
                def _():
                    copy = pltpu.make_async_copy(source, held, sem)
                    copy.start()
                    copy.wait()

            shifted_block(info, info[3 + at], info[1 + half], held, queries, acc, sums, peak)
            return carry

        lax.fori_loop(0, earlier + blocks, block_step, 0)

    for head in range(GROUP):
        rows = pl.ds(head * TOK, TOK)
        total = jnp.sum(sums[rows, :], axis=1, keepdims=True)
        out[rows, :] = (acc[rows, :] / jnp.where(total > 0, total, 1.0)).astype(out.dtype)
        level = jnp.where(total > 0, peak[rows, :] + jnp.log2(jnp.where(total > 0, total, 1.0)), NEG)
        levels[pl.ds(head, 1), :] = jnp.transpose(level)[0:1, :]
    high = levels[...].astype(jnp.bfloat16)
    rest = levels[...] - high.astype(jnp.float32)
    middle = rest.astype(jnp.bfloat16)
    low = (rest - middle.astype(jnp.float32)).astype(jnp.bfloat16)
    out[pl.ds(ROWS, STATS), :] = jnp.concatenate([high, middle, low, jnp.zeros_like(low)], 0)


def unpack_levels(packed):
    pieces = [packed[pl.ds(ROWS, STATS), :].astype(jnp.float32)]
    return pieces[0][0:8] + pieces[0][8:16] + pieces[0][16:24]


def whole(shape):
    return pl.BlockSpec(shape, lambda *_: (0,) * len(shape))


SMEM = pl.BlockSpec(memory_space=pltpu.SMEM)
STATE = jax.ShapeDtypeStruct((ROWS, 128), jnp.float32)


def attend_cost(halves, blocks):
    return pl.CostEstimate(
        flops=blocks * 4 * halves * ROWS * BLOCK * HEAD_DIM * 2,
        bytes_accessed=blocks * BLOCK * 512 + 4 * halves * ROWS * 512,
        transcendentals=blocks * halves * ROWS * BLOCK,
    )


def attend(info, queries, halves, first_block, kvs, state, name):
    blocks, count = len(kvs), len(halves)
    return pl.pallas_call(
        functools.partial(attend_kernel, halves, first_block, blocks, not state),
        out_shape=[STATE] * (2 * count),
        in_specs=[SMEM]
        + [whole(q.shape) for q in queries]
        + [whole(kv.shape) for kv in kvs]
        + [whole(STATE.shape)] * len(state),
        out_specs=[whole(STATE.shape)] * (2 * count),
        scratch_shapes=[
            pltpu.VMEM((count * ROWS, HEAD_DIM), jnp.bfloat16),
            pltpu.VMEM((count * ROWS, 128), jnp.float32),
            pltpu.VMEM((count * ROWS, 128), jnp.float32),
            pltpu.VMEM((2 * blocks * TOK, HEAD_DIM), jnp.bfloat16),
        ],
        compiler_params=pltpu.CompilerParams(vmem_limit_bytes=VMEM_LIMIT),
        cost_estimate=attend_cost(count, blocks),
        name=name,
    )(info, *queries, *kvs, *state)


def attend_last(info, q, half, earlier, kvs, state, name):
    blocks = len(kvs)
    packed = jax.ShapeDtypeStruct((ROWS + STATS, HEAD_DIM), jnp.bfloat16)
    return pl.pallas_call(
        functools.partial(last_kernel, half, len(earlier), blocks),
        grid=(1,),
        out_shape=packed,
        in_specs=[SMEM, whole(q.shape)]
        + [pl.BlockSpec(memory_space=pl.ANY)] * len(earlier)
        + [whole(kv.shape) for kv in kvs]
        + [whole(STATE.shape)] * 2,
        out_specs=whole(packed.shape),
        scratch_shapes=[
            pltpu.VMEM((ROWS, HEAD_DIM), jnp.bfloat16),
            pltpu.VMEM((ROWS, 128), jnp.float32),
            pltpu.VMEM((ROWS, 128), jnp.float32),
            pltpu.VMEM((2 * blocks * TOK, HEAD_DIM), jnp.bfloat16),
            pltpu.VMEM((ROWS, 128), jnp.float32),
            pltpu.VMEM((2 * BLOCK, HEAD_DIM), jnp.bfloat16),
            pltpu.VMEM((GROUP, TOK), jnp.float32),
            pltpu.SemaphoreType.DMA(()),
        ],
        compiler_params=pltpu.CompilerParams(vmem_limit_bytes=VMEM_LIMIT),
        cost_estimate=attend_cost(1, blocks),
        name=name,
    )(info, q, *earlier, *kvs, *state)


def softmax_rows(s, seen):
    s = jnp.where(seen, s, NEG)
    return s, jnp.max(s, axis=1, keepdims=True)


def spread(rows, flat):
    for head in range(GROUP):
        piece = rows[:, pl.ds(head * HEAD_DIM, HEAD_DIM)].astype(jnp.float32)
        flat[pl.ds(head, rows.shape[0], stride=GROUP), :] = piece


def gather_heads(flat, rows):
    for head in range(GROUP):
        piece = flat[pl.ds(head, rows.shape[0], stride=GROUP), :]
        rows[:, pl.ds(head * HEAD_DIM, HEAD_DIM)] = piece.astype(rows.dtype)


def heads_at(row):
    return pl.ds(pl.multiple_of(row * GROUP, GROUP), GROUP)


def relative(to, place):
    x_steps = (to // 2 - place // 2 + 4) % 4
    return x_steps * 4 + ((to // 8) ^ (place // 8)) * 2 + ((to % 2) ^ (place % 2))


def rows_kernel(
    dec_len, owner, hand_count, place, dec_q, dec_k, dec_v, hand_q, cache_k, cache_v, hand_k, hand_v,
    dec_out, slot_0, slot_1, slot_2, slot_3,
    dec_rows, hand_rows, dec_sums, slot_sums, cache_ks, cache_vs, hand_ks, hand_vs, sems, taken,
):
    rows, blocks = cache_k.shape[0], hand_k.shape[0]
    copies = [pltpu.make_async_copy(hand_k, hand_ks, sems.at[0]), pltpu.make_async_copy(hand_v, hand_vs, sems.at[1])]
    for row in range(rows):
        copies.append(pltpu.make_async_copy(cache_k.at[row], cache_ks.at[row], sems.at[2 + 2 * row]))
        copies.append(pltpu.make_async_copy(cache_v.at[row], cache_vs.at[row], sems.at[3 + 2 * row]))
    for copy in copies:
        copy.start()
    spread(dec_q, dec_rows)
    spread(hand_q, hand_rows)
    dec_sums[...] = jnp.zeros_like(dec_sums)
    slot_sums[...] = jnp.zeros_like(slot_sums)
    for at in range(taken.shape[0]):
        taken[at] = 0
    copies[0].wait()
    copies[1].wait()
    queries = [hand_rows[pl.ds(at * GROUP, GROUP), :].astype(jnp.bfloat16) for at in range(blocks)]
    s = jnp.concatenate([dot_t(queries[at], hand_ks[at]) for at in range(blocks)], 0) * SCALE
    count = jnp.zeros(s.shape, jnp.int32)
    block_of = lax.broadcasted_iota(jnp.int32, s.shape, 0) // GROUP
    for at in range(blocks):
        count = jnp.where(block_of == at, hand_count[at], count)
    seen = lax.broadcasted_iota(jnp.int32, s.shape, 1) < count
    s, top = softmax_rows(s, seen)
    p = jnp.where(seen, jnp.exp2(s - top), 0.0)
    total = jnp.sum(p, axis=1, keepdims=True)
    summed = [
        dot(p[at * GROUP : (at + 1) * GROUP].astype(jnp.bfloat16), hand_vs[at]) for at in range(blocks)
    ]
    results = jnp.concatenate(summed, 0) / jnp.where(total > 0, total, 1.0)
    for at in range(blocks):
        to = owner[at]
        slot = relative(to, place[0]) * MOST + taken[to]
        taken[to] = taken[to] + 1
        slot_sums[heads_at(slot), :] = results[at * GROUP : (at + 1) * GROUP]
    for copy in copies[2:]:
        copy.wait()
    queries = [dec_rows[pl.ds(row * GROUP, GROUP), :].astype(jnp.bfloat16) for row in range(rows)]
    s = jnp.concatenate([dot_t(queries[row], cache_ks[row]) for row in range(rows)], 0) * SCALE
    keys = jnp.concatenate(
        [jnp.broadcast_to(dec_k[row : row + 1, :].astype(jnp.float32), (GROUP, HEAD_DIM)) for row in range(rows)], 0
    )
    values = jnp.concatenate(
        [jnp.broadcast_to(dec_v[row : row + 1, :].astype(jnp.float32), (GROUP, HEAD_DIM)) for row in range(rows)], 0
    )
    own = jnp.sum(dec_rows[...] * keys, axis=1, keepdims=True) * SCALE
    row_of = lax.broadcasted_iota(jnp.int32, (rows * GROUP, 1), 0) // GROUP
    count = jnp.zeros((rows * GROUP, 1), jnp.int32)
    for row in range(rows):
        count = jnp.where(row_of == row, dec_len[row], count)
    seen = lax.broadcasted_iota(jnp.int32, s.shape, 1) < count
    s, top = softmax_rows(s, seen)
    top = jnp.maximum(top, own)
    p = jnp.where(seen, jnp.exp2(s - top), 0.0)
    own = jnp.exp2(own - top)
    total = jnp.sum(p, axis=1, keepdims=True) + own
    p = p.astype(jnp.bfloat16)
    summed = jnp.concatenate([dot(p[row * GROUP : (row + 1) * GROUP], cache_vs[row]) for row in range(rows)], 0)
    summed = summed + own.astype(jnp.bfloat16).astype(jnp.float32) * values
    dec_sums[pl.ds(0, rows * GROUP), :] = summed / total
    gather_heads(dec_sums, dec_out)
    for step, out in enumerate((slot_0, slot_1, slot_2, slot_3)):
        gather_heads(slot_sums.at[pl.ds(step * 8 * GROUP, 8 * GROUP)], out)


def attend_rows(dec_len, owner, hand_count, place, dec_q, dec_k, dec_v, hand_q, cache_k, cache_v, hand_k, hand_v, owners):
    rows = cache_k.shape[0]
    blocks = hand_k.shape[0]
    width = dec_q.shape[1]
    return pl.pallas_call(
        rows_kernel,
        out_shape=(
            jax.ShapeDtypeStruct((16, width), jnp.bfloat16),
            *[jax.ShapeDtypeStruct((owners * MOST // 4, width), jnp.float32)] * 4,
        ),
        in_specs=[SMEM] * 4
        + [whole(a.shape) for a in (dec_q, dec_k, dec_v, hand_q)]
        + [pl.BlockSpec(memory_space=pl.ANY)] * 4,
        out_specs=(whole((16, width)), *[whole((owners * MOST // 4, width))] * 4),
        scratch_shapes=[
            pltpu.VMEM((rows * GROUP, HEAD_DIM), jnp.float32),
            pltpu.VMEM((blocks * GROUP, HEAD_DIM), jnp.float32),
            pltpu.VMEM((16 * GROUP, HEAD_DIM), jnp.float32),
            pltpu.VMEM((owners * MOST * GROUP, HEAD_DIM), jnp.float32),
            pltpu.VMEM(cache_k.shape, jnp.bfloat16),
            pltpu.VMEM(cache_v.shape, jnp.bfloat16),
            pltpu.VMEM(hand_k.shape, jnp.bfloat16),
            pltpu.VMEM(hand_v.shape, jnp.bfloat16),
            pltpu.SemaphoreType.DMA((2 + 2 * rows,)),
            pltpu.SMEM((owners,), jnp.int32),
        ],
        compiler_params=pltpu.CompilerParams(vmem_limit_bytes=56 * 2**20),
        cost_estimate=pl.CostEstimate(flops=10**6, bytes_accessed=10**4, transcendentals=0),
        name="rows",
    )(dec_len, owner, hand_count, place, dec_q, dec_k, dec_v, hand_q, cache_k, cache_v, hand_k, hand_v)


def part_kernel(count, rows, *refs):
    pieces, (keep, send) = refs[:count], refs[count:]
    at = 0
    for piece in pieces:
        for start in range(0, piece.shape[0], 2 * rows):
            keep[pl.ds(at, rows), :] = piece[pl.ds(start, rows), :]
            send[pl.ds(at, rows), :] = piece[pl.ds(start + rows, rows), :]
            at += rows


def part_rows(pieces, rows, name):
    half = sum(piece.shape[0] for piece in pieces) // 2
    out = jax.ShapeDtypeStruct((half, pieces[0].shape[1]), pieces[0].dtype)
    return pl.pallas_call(
        functools.partial(part_kernel, len(pieces), rows),
        out_shape=(out, out),
        in_specs=[whole(piece.shape) for piece in pieces],
        out_specs=(whole(out.shape),) * 2,
        compiler_params=pltpu.CompilerParams(vmem_limit_bytes=8 * 2**20),
        name=name,
    )(*pieces)


def join_kernel(*refs):
    sources, out, sems = refs[:4], refs[4], refs[5]
    copies = []
    at = 0
    for n, source in enumerate(sources):
        copies.append(pltpu.make_async_copy(source, out.at[pl.ds(at, source.shape[0])], sems.at[n]))
        at += source.shape[0]
    for copy in copies:
        copy.start()
    for copy in copies:
        copy.wait()


def join(*pieces):
    rows = sum(piece.shape[0] for piece in pieces)
    return pl.pallas_call(
        join_kernel,
        out_shape=jax.ShapeDtypeStruct((rows, HEAD_DIM), jnp.bfloat16),
        in_specs=[pl.BlockSpec(memory_space=pl.ANY)] * 4,
        out_specs=whole((rows, HEAD_DIM)),
        scratch_shapes=[pltpu.SemaphoreType.DMA((4,))],
        compiler_params=pltpu.CompilerParams(vmem_limit_bytes=56 * 2**20),
        cost_estimate=pl.CostEstimate(flops=0, bytes_accessed=rows * 512, transcendentals=0),
        name="join",
    )(*pieces)


def column(row):
    return jnp.transpose(jnp.broadcast_to(row, (TOK, TOK)))


def slot_order(place):
    count = 32
    to = lax.broadcasted_iota(jnp.int32, (count, count), 0)
    at = lax.broadcasted_iota(jnp.int32, (count, count), 1)
    core, high, steps, rank = at // 16, (at // 8) % 2, (at // 2) % 4, at % 2
    x = (place // 2 - steps + 4) % 4
    source = ((place // 8) ^ high) * 8 + x * 2 + ((place % 2) ^ core)
    return jnp.where(to == source * 2 + rank, 1.0, 0.0).astype(jnp.bfloat16)


def project_kernel(place, order, mine, other, new_a, new_b, dec, weight, *refs):
    outs, attn = refs[:-1], refs[-1]

    @pl.when(pl.program_id(0) == 0)
    def _():
        a_levels, b_levels = unpack_levels(mine), unpack_levels(other)
        top = jnp.maximum(a_levels, b_levels)
        wa, wb = jnp.exp2(a_levels - top), jnp.exp2(b_levels - top)
        wa, wb = wa / (wa + wb), wb / (wa + wb)
        for head in range(GROUP):
            rows = pl.ds(head * TOK, TOK)
            a, b = mine[rows, :].astype(jnp.float32), other[rows, :].astype(jnp.float32)
            mixed = a * column(wa[head : head + 1, :]) + b * column(wb[head : head + 1, :])
            attn[pl.ds(0, TOK), pl.ds(head * HEAD_DIM, HEAD_DIM)] = mixed.astype(attn.dtype)
        new = jnp.concatenate([new_a[...], new_b[...]], 0).astype(jnp.bfloat16)
        attn[pl.ds(TOK, 32), :] = dot(slot_order(place[0]), new).astype(attn.dtype)
        attn[pl.ds(TOK + 32, 16), :] = dec[...]

    result = dot(attn[...], weight[...]).astype(jnp.bfloat16)
    for step, out in enumerate(outs):

        @pl.when(pl.program_id(0) == step)
        def _():
            out[...] = result[: out.shape[0]]


def project(place, order, inputs, weight, rows):
    depth, width = weight.shape
    steps = order.shape[0]
    columns = width // steps
    outs = [jax.ShapeDtypeStruct((rows, columns), jnp.bfloat16)] * steps
    return pl.pallas_call(
        project_kernel,
        grid_spec=pltpu.PrefetchScalarGridSpec(
            num_scalar_prefetch=2,
            grid=(steps,),
            in_specs=[whole(a.shape) for a in inputs]
            + [pl.BlockSpec((depth, columns), lambda i, place, order: (0, order[i]))],
            out_specs=[whole(out.shape) for out in outs],
            scratch_shapes=[pltpu.VMEM((TOK + 32 + 16, depth), jnp.bfloat16)],
        ),
        out_shape=outs,
        compiler_params=pltpu.CompilerParams(vmem_limit_bytes=VMEM_LIMIT),
        cost_estimate=pl.CostEstimate(flops=2 * rows * depth * width, bytes_accessed=2 * depth * width, transcendentals=0),
        name="project",
    )(place, order, *inputs, weight)


def total_of(*parts):
    total = parts[0].astype(jnp.float32)
    for part in parts[1:]:
        total = total + part.astype(jnp.float32)
    return total.astype(jnp.bfloat16)


def total_kernel(*refs):
    parts, outs = refs[:-3], refs[-3:]
    total = parts[0][...].astype(jnp.float32)
    for part in parts[1:]:
        total = total + part[...].astype(jnp.float32)
    total = total.astype(jnp.bfloat16)
    at = 0
    for out in outs:
        out[...] = total[at : at + out.shape[0]]
        at += out.shape[0]


def add_up(parts, rows):
    width = parts[0].shape[1]
    return pl.pallas_call(
        total_kernel,
        out_shape=[jax.ShapeDtypeStruct((count, width), jnp.bfloat16) for count in rows],
        in_specs=[whole(part.shape) for part in parts],
        out_specs=[whole((count, width)) for count in rows],
        compiler_params=pltpu.CompilerParams(vmem_limit_bytes=VMEM_LIMIT),
        cost_estimate=pl.CostEstimate(flops=0, bytes_accessed=len(parts) * sum(rows) * width * 2, transcendentals=0),
        name="add_up",
    )(*parts)


def local(
    stretch_start,
    stretch_q,
    stretch_k,
    stretch_v,
    prefix_k,
    prefix_v,
    dec_len,
    dec_q,
    dec_k,
    dec_v,
    cache_k,
    cache_v,
    hand_owner,
    hand_count,
    hand_q,
    hand_k,
    hand_v,
    out_weight,
):
    place = lax.axis_index("ctx")
    me = lax.axis_index("tp")
    y, x, c = place // 8, (place // 2) % 4, place % 2

    b0 = join(prefix_k, stretch_k, prefix_v, stretch_v)
    b1 = lax.ppermute(b0, "ctx", X_UP)
    b2 = lax.ppermute(b0, "ctx", X_DOWN)
    c0 = lax.ppermute(b0, "ctx", CORE_SWAP)
    other_q = lax.ppermute(stretch_q, "ctx", Y_SWAP)
    up, down, two = (x + 1) % 4, (x + 3) % 4, (x + 2) % 4
    info = jnp.stack(
        [
            stretch_start[0],
            place,
            ctx_index(1 - y, x, c),
            place,
            ctx_index(y, x, 1 - c),
            ctx_index(y, down, c),
            ctx_index(y, down, 1 - c),
            ctx_index(y, up, c),
            ctx_index(y, up, 1 - c),
            ctx_index(y, two, c),
            ctx_index(y, two, 1 - c),
        ]
    ).astype(jnp.int32)

    h, z = me // 4, me % 4
    order = jnp.stack(
        [
            tp_index(1 - h, z + 2),
            tp_index(1 - h, z + 1),
            tp_index(1 - h, z + 3),
            tp_index(h, z + 1),
            tp_index(h, z + 3),
            tp_index(h, z + 2),
            tp_index(1 - h, z),
            me,
        ]
    ).astype(jnp.int32)
    ctx_count = lax.axis_size("ctx")
    at_place = place[None].astype(jnp.int32)
    info, order, at_place = lax.optimization_barrier((info, order, at_place))
    dec_attn, *slots = attend_rows(
        dec_len, hand_owner[:, 0], hand_count, at_place, dec_q, dec_k, dec_v, hand_q,
        cache_k, cache_v, hand_k, hand_v, ctx_count,
    )
    info, order, other_q, dec_attn = lax.optimization_barrier((info, order, other_q, dec_attn))
    own = attend(info, [stretch_q], (0,), 0, [b0, c0], [], "attend_own")
    info, b0_later, b1, b2, own = lax.optimization_barrier((info, b0, b1, b2, own))
    b4 = lax.ppermute(b0_later, "ctx", X_TWO)
    c1 = lax.ppermute(b1, "ctx", CORE_SWAP)
    c2 = lax.ppermute(b2, "ctx", CORE_SWAP)
    theirs = attend(info, [other_q], (1,), 0, [b0, c0], [], "attend_other")

    state = attend(info, [stretch_q, other_q], (0, 1), 2, [b1, c1, b2, c2], own + theirs, "attend_both")

    slots, state, b4 = lax.optimization_barrier((slots, state, b4))
    c4 = lax.ppermute(b4, "ctx", CORE_SWAP)
    slots[1] = lax.ppermute(slots[1], "ctx", X_UP)
    slots[2] = lax.ppermute(slots[2], "ctx", X_TWO)
    slots[3] = lax.ppermute(slots[3], "ctx", X_DOWN)
    before = [b0, c0, b1, c1, b2, c2]
    give = attend_last(info, other_q, 1, before, [b4, c4], state[2:], "attend_give")
    slots, give = lax.optimization_barrier((slots, give))
    other = lax.ppermute(give, "ctx", Y_SWAP)
    keep, send = part_rows(slots, 4, "part_y")
    got = lax.ppermute(send, "ctx", Y_SWAP)
    mine = attend_last(info, stretch_q, 0, before, [b4, c4], state[:2], "attend_keep")
    keep, got, mine = lax.optimization_barrier((keep, got, mine))
    new_a, send = part_rows([keep, got], 2, "part_core")
    new_b = lax.ppermute(send, "ctx", CORE_SWAP)

    counts = (TOK, ctx_count * MOST, dec_q.shape[0])
    rows = sum(counts)
    cross, above_far, below_far, above, below, two, across, own = project(
        at_place, order, (mine, other, new_a, new_b, dec_attn), out_weight, rows
    )
    cross = lax.ppermute(cross, "tp", H_SWAP)
    above_far = lax.ppermute(above_far, "tp", Z_UP)
    below_far = lax.ppermute(below_far, "tp", Z_DOWN)
    above = lax.ppermute(above, "tp", Z_UP)
    below = lax.ppermute(below, "tp", Z_DOWN)
    two = lax.ppermute(total_of(two, cross), "tp", Z_TWO)
    across = lax.ppermute(total_of(across, above_far, below_far), "tp", H_SWAP)
    stretch_out, new_out, dec_out = add_up([own, above, below, two, across], counts)
    return stretch_out, dec_out, new_out


def solution(mesh):
    in_specs = (
        P(),
        P("ctx", "tp"),
        P("ctx", "tp"),
        P("ctx", "tp"),
        P("ctx", "tp"),
        P("ctx", "tp"),
        P("ctx"),
        P("ctx", "tp"),
        P("ctx", "tp"),
        P("ctx", "tp"),
        P("ctx", None, "tp"),
        P("ctx", None, "tp"),
        P("ctx", None),
        P("ctx"),
        P("ctx", "tp"),
        P("ctx", None, "tp"),
        P("ctx", None, "tp"),
        P("tp", None),
    )
    out_specs = (P("ctx", "tp"), P("ctx", "tp"), P("ctx", "tp"))
    return jax.shard_map(local, mesh=mesh, in_specs=in_specs, out_specs=out_specs, check_vma=False)
```

```python
import functools
import math

import jax
import jax.numpy as jnp
from jax import lax
from jax.experimental import pallas as pl
from jax.experimental.pallas import tpu as pltpu
from jax.sharding import PartitionSpec as P

HEAD_DIM = 128
MOST = 2
GROUP = 8
TOK = 128
PRE = 1024
BLOCK = PRE + TOK
ROWS = GROUP * TOK
TILE = 512
SUB = 256
NEG = -1e30
SCALE = math.log2(math.e) / math.sqrt(HEAD_DIM)
LOW, HIGH = 2.0**-60, 2.0**100
VMEM_LIMIT = 24 * 2**20
STATS = 32


def dot_t(a, b):
    return lax.dot_general(a, b, (((1,), (1,)), ((), ())), preferred_element_type=jnp.float32)


def dot(a, b):
    return jnp.dot(a, b, preferred_element_type=jnp.float32)


def ctx_index(y, x, c):
    return y * 8 + x * 2 + c


def ctx_perm(move):
    return [
        (ctx_index(y, x, c), ctx_index(*move(y, x, c)))
        for y in range(2)
        for x in range(4)
        for c in range(2)
    ]


X_UP = ctx_perm(lambda y, x, c: (y, (x + 1) % 4, c))
X_DOWN = ctx_perm(lambda y, x, c: (y, (x + 3) % 4, c))
X_TWO = ctx_perm(lambda y, x, c: (y, (x + 2) % 4, c))
Y_SWAP = ctx_perm(lambda y, x, c: (1 - y, x, c))
CORE_SWAP = ctx_perm(lambda y, x, c: (y, x, 1 - c))


def tp_index(h, z):
    return h * 4 + z % 4


def tp_perm(move):
    return [(tp_index(h, z), tp_index(*move(h, z))) for h in range(2) for z in range(4)]


Z_UP = tp_perm(lambda h, z: (h, z + 1))
Z_DOWN = tp_perm(lambda h, z: (h, z + 3))
Z_TWO = tp_perm(lambda h, z: (h, z + 2))
H_SWAP = tp_perm(lambda h, z: (1 - h, z))


def lane_sums(p):
    total = p[:, 0:128]
    for at in range(128, p.shape[1], 128):
        total = total + p[:, at : at + 128]
    return total


def stack_queries(q_refs, queries):
    for half, ref in enumerate(q_refs):
        for head in range(GROUP):
            queries[pl.ds(half * ROWS + head * TOK, TOK), :] = ref[:, pl.ds(head * HEAD_DIM, HEAD_DIM)]


def add_block(info, block_at, kv, queries, acc, sums, halves):
    prefix_end = info[0]
    chunk = info[3 + block_at]
    count = jnp.clip(prefix_end - chunk * PRE, 0, PRE)

    @pl.when(count == PRE)
    def _():
        for tile in range(len(halves) * ROWS // TILE):
            rows = pl.ds(tile * TILE, TILE)
            for at in range(0, PRE, 512):
                p = jnp.exp2(dot_t(queries[rows, :], kv[pl.ds(at, 512), :]) * SCALE)
                acc[rows, :] += dot(p.astype(jnp.bfloat16), kv[pl.ds(BLOCK + at, 512), :])
                sums[rows, :] += lane_sums(p)

    @pl.when(jnp.logical_and(count > 0, count < PRE))
    def _():
        def step(at, carry):
            start = pl.multiple_of(at * SUB, SUB)
            columns = start + lax.broadcasted_iota(jnp.int32, (TILE, SUB), 1)
            for tile in range(len(halves) * ROWS // TILE):
                rows = pl.ds(tile * TILE, TILE)
                s = dot_t(queries[rows, :], kv[pl.ds(start, SUB), :]) * SCALE
                p = jnp.where(columns < count, jnp.exp2(s), 0.0)
                acc[rows, :] += dot(p.astype(jnp.bfloat16), kv[pl.ds(BLOCK + start, SUB), :])
                sums[rows, :] += lane_sums(p)
            return carry

        lax.fori_loop(0, (count + SUB - 1) // SUB, step, 0)


def add_tokens(info, first_block, kvs, queries, acc, sums, halves, near):
    count = len(kvs)
    width = count * TOK
    for at, kv in enumerate(kvs):
        near[pl.ds(at * TOK, TOK), :] = kv[pl.ds(PRE, TOK), :]
        near[pl.ds(width + at * TOK, TOK), :] = kv[pl.ds(BLOCK + PRE, TOK), :]
    for at_half, half in enumerate(halves):
        place = info[1 + half]
        seen_from = [place - info[3 + first_block + at] for at in range(count)]
        some = functools.reduce(jnp.maximum, seen_from)

        @pl.when(some >= 0)
        def _():
            column = lax.broadcasted_iota(jnp.int32, (1, width), 1)
            start = jnp.zeros((1, width), jnp.int32)
            for at in range(count):
                least = jnp.where(seen_from[at] > 0, -TOK, jnp.where(seen_from[at] == 0, 0, TOK))
                start = jnp.where(column // TOK == at, least, start)
            start = start + column % TOK
            token = lax.broadcasted_iota(jnp.int32, (TILE, width), 0) % TOK
            seen = start <= token
            for tile in range(ROWS // TILE):
                rows = pl.ds(at_half * ROWS + tile * TILE, TILE)
                s = dot_t(queries[rows, :], near[pl.ds(0, width), :]) * SCALE
                p = jnp.where(seen, jnp.exp2(s), 0.0)
                acc[rows, :] += dot(p.astype(jnp.bfloat16), near[pl.ds(width, width), :])
                sums[rows, :] += lane_sums(p)


def shifted_step(rows, s, seen, values, queries, acc, sums, peak):
    s = jnp.where(seen, s, NEG)
    before = peak[rows, :]
    now = jnp.maximum(before, jnp.max(s, axis=1, keepdims=True))
    p = jnp.where(seen, jnp.exp2(s - now[:, 0:1]), 0.0)
    fade = jnp.exp2(before - now)
    acc[rows, :] = acc[rows, :] * fade + dot(p.astype(jnp.bfloat16), values)
    sums[rows, :] = sums[rows, :] * fade + lane_sums(p)
    peak[rows, :] = now


def shifted_block(info, chunk, place, kv, queries, acc, sums, peak):
    count = jnp.clip(info[0] - chunk * PRE, 0, PRE)
    tile_rows = 256

    def tile_step(tile, carry):
        rows = pl.ds(pl.multiple_of(tile * tile_rows, tile_rows), tile_rows)

        def step(at, carry):
            start = pl.multiple_of(at * SUB, SUB)
            columns = start + lax.broadcasted_iota(jnp.int32, (tile_rows, SUB), 1)
            s = dot_t(queries[rows, :], kv[pl.ds(start, SUB), :]) * SCALE
            shifted_step(rows, s, columns < count, kv[pl.ds(BLOCK + start, SUB), :], queries, acc, sums, peak)
            return carry

        lax.fori_loop(0, (count + SUB - 1) // SUB, step, 0)

        @pl.when(chunk <= place)
        def _():
            token = lax.broadcasted_iota(jnp.int32, (tile_rows, TOK), 0) % TOK
            key = lax.broadcasted_iota(jnp.int32, (tile_rows, TOK), 1)
            seen = key <= token + jnp.where(chunk < place, TOK, 0)
            s = dot_t(queries[rows, :], kv[pl.ds(PRE, TOK), :]) * SCALE
            shifted_step(rows, s, seen, kv[pl.ds(BLOCK + PRE, TOK), :], queries, acc, sums, peak)

        return carry

    lax.fori_loop(0, ROWS // tile_rows, tile_step, 0)


def attend_kernel(halves, first_block, blocks, starts, info, *refs):
    count = len(halves)
    q_refs, refs = refs[:count], refs[count:]
    kvs, refs = refs[:blocks], refs[blocks:]
    if not starts:
        before, refs = refs[: 2 * count], refs[2 * count :]
    after, (queries, acc, sums, near) = refs[: 2 * count], refs[2 * count :]
    stack_queries(q_refs, queries)
    if starts:
        acc[...] = jnp.zeros_like(acc)
        sums[...] = jnp.zeros_like(sums)
    else:
        for at in range(count):
            acc[pl.ds(at * ROWS, ROWS), :] = before[2 * at][...]
            sums[pl.ds(at * ROWS, ROWS), :] = before[2 * at + 1][...]
    for at in range(blocks):
        add_block(info, first_block + at, kvs[at], queries, acc, sums, halves)
    add_tokens(info, first_block, kvs, queries, acc, sums, halves, near)
    for at in range(count):
        after[2 * at][...] = acc[pl.ds(at * ROWS, ROWS), :]
        after[2 * at + 1][...] = sums[pl.ds(at * ROWS, ROWS), :]


def last_kernel(half, earlier, blocks, info, q_ref, *refs):
    earlier_kvs, refs = refs[:earlier], refs[earlier:]
    kvs, refs = refs[:blocks], refs[blocks:]
    acc_in, sums_in, out, queries, acc, sums, near, peak, held, levels, sem = refs
    stack_queries((q_ref,), queries)
    acc[...] = acc_in[...]
    sums[...] = sums_in[...]
    for at in range(blocks):
        add_block(info, earlier + at, kvs[at], queries, acc, sums, (half,))
    add_tokens(info, earlier, kvs, queries, acc, sums, (half,), near)
    peak[...] = jnp.zeros_like(peak)
    has_keys = jnp.int32(0)
    for at in range(earlier + blocks):
        chunk = info[3 + at]
        some = jnp.logical_or(info[0] > chunk * PRE, chunk <= info[1 + half])
        has_keys = jnp.where(some, 1, has_keys)
    total = jnp.sum(sums[...], axis=1, keepdims=True)
    inside = jnp.where(jnp.logical_and(total >= LOW, total <= HIGH), 1.0, 0.0)

    @pl.when(jnp.logical_and(has_keys > 0, jnp.min(inside) < 0.5))
    def _():
        acc[...] = jnp.zeros_like(acc)
        sums[...] = jnp.zeros_like(sums)
        peak[...] = jnp.full_like(peak, NEG)

        def block_step(at, carry):
            for one in range(earlier + blocks):
                source = earlier_kvs[one] if one < earlier else kvs[one - earlier]

                @pl.when(at == one)
                def _():
                    copy = pltpu.make_async_copy(source, held, sem)
                    copy.start()
                    copy.wait()

            shifted_block(info, info[3 + at], info[1 + half], held, queries, acc, sums, peak)
            return carry

        lax.fori_loop(0, earlier + blocks, block_step, 0)

    for head in range(GROUP):
        rows = pl.ds(head * TOK, TOK)
        total = jnp.sum(sums[rows, :], axis=1, keepdims=True)
        out[rows, :] = (acc[rows, :] / jnp.where(total > 0, total, 1.0)).astype(out.dtype)
        level = jnp.where(total > 0, peak[rows, :] + jnp.log2(jnp.where(total > 0, total, 1.0)), NEG)
        levels[pl.ds(head, 1), :] = jnp.transpose(level)[0:1, :]
    high = levels[...].astype(jnp.bfloat16)
    rest = levels[...] - high.astype(jnp.float32)
    middle = rest.astype(jnp.bfloat16)
    low = (rest - middle.astype(jnp.float32)).astype(jnp.bfloat16)
    out[pl.ds(ROWS, STATS), :] = jnp.concatenate([high, middle, low, jnp.zeros_like(low)], 0)


def unpack_levels(packed):
    pieces = [packed[pl.ds(ROWS, STATS), :].astype(jnp.float32)]
    return pieces[0][0:8] + pieces[0][8:16] + pieces[0][16:24]


def whole(shape):
    return pl.BlockSpec(shape, lambda *_: (0,) * len(shape))


SMEM = pl.BlockSpec(memory_space=pltpu.SMEM)
STATE = jax.ShapeDtypeStruct((ROWS, 128), jnp.float32)


def attend_cost(halves, blocks):
    return pl.CostEstimate(
        flops=blocks * 4 * halves * ROWS * BLOCK * HEAD_DIM * 2,
        bytes_accessed=blocks * BLOCK * 512 + 4 * halves * ROWS * 512,
        transcendentals=blocks * halves * ROWS * BLOCK,
    )


def attend(info, queries, halves, first_block, kvs, state, name):
    blocks, count = len(kvs), len(halves)
    return pl.pallas_call(
        functools.partial(attend_kernel, halves, first_block, blocks, not state),
        out_shape=[STATE] * (2 * count),
        in_specs=[SMEM]
        + [whole(q.shape) for q in queries]
        + [whole(kv.shape) for kv in kvs]
        + [whole(STATE.shape)] * len(state),
        out_specs=[whole(STATE.shape)] * (2 * count),
        scratch_shapes=[
            pltpu.VMEM((count * ROWS, HEAD_DIM), jnp.bfloat16),
            pltpu.VMEM((count * ROWS, 128), jnp.float32),
            pltpu.VMEM((count * ROWS, 128), jnp.float32),
            pltpu.VMEM((2 * blocks * TOK, HEAD_DIM), jnp.bfloat16),
        ],
        compiler_params=pltpu.CompilerParams(vmem_limit_bytes=VMEM_LIMIT),
        cost_estimate=attend_cost(count, blocks),
        name=name,
    )(info, *queries, *kvs, *state)


def attend_last(info, q, half, earlier, kvs, state, name):
    blocks = len(kvs)
    packed = jax.ShapeDtypeStruct((ROWS + STATS, HEAD_DIM), jnp.bfloat16)
    return pl.pallas_call(
        functools.partial(last_kernel, half, len(earlier), blocks),
        grid=(1,),
        out_shape=packed,
        in_specs=[SMEM, whole(q.shape)]
        + [pl.BlockSpec(memory_space=pl.ANY)] * len(earlier)
        + [whole(kv.shape) for kv in kvs]
        + [whole(STATE.shape)] * 2,
        out_specs=whole(packed.shape),
        scratch_shapes=[
            pltpu.VMEM((ROWS, HEAD_DIM), jnp.bfloat16),
            pltpu.VMEM((ROWS, 128), jnp.float32),
            pltpu.VMEM((ROWS, 128), jnp.float32),
            pltpu.VMEM((2 * blocks * TOK, HEAD_DIM), jnp.bfloat16),
            pltpu.VMEM((ROWS, 128), jnp.float32),
            pltpu.VMEM((2 * BLOCK, HEAD_DIM), jnp.bfloat16),
            pltpu.VMEM((GROUP, TOK), jnp.float32),
            pltpu.SemaphoreType.DMA(()),
        ],
        compiler_params=pltpu.CompilerParams(vmem_limit_bytes=VMEM_LIMIT),
        cost_estimate=attend_cost(1, blocks),
        name=name,
    )(info, q, *earlier, *kvs, *state)


def softmax_rows(s, seen):
    s = jnp.where(seen, s, NEG)
    return s, jnp.max(s, axis=1, keepdims=True)


def spread(rows, flat):
    for head in range(GROUP):
        piece = rows[:, pl.ds(head * HEAD_DIM, HEAD_DIM)].astype(jnp.float32)
        flat[pl.ds(head, rows.shape[0], stride=GROUP), :] = piece


def gather_heads(flat, rows):
    for head in range(GROUP):
        piece = flat[pl.ds(head, rows.shape[0], stride=GROUP), :]
        rows[:, pl.ds(head * HEAD_DIM, HEAD_DIM)] = piece.astype(rows.dtype)


def heads_at(row):
    return pl.ds(pl.multiple_of(row * GROUP, GROUP), GROUP)


def relative(to, place):
    x_steps = (to // 2 - place // 2 + 4) % 4
    return x_steps * 4 + ((to // 8) ^ (place // 8)) * 2 + ((to % 2) ^ (place % 2))


def rows_kernel(
    dec_len, owner, hand_count, place, dec_q, dec_k, dec_v, hand_q, cache_k, cache_v, hand_k, hand_v,
    dec_out, slot_0, slot_1, slot_2, slot_3,
    dec_rows, hand_rows, dec_sums, slot_sums, cache_ks, cache_vs, hand_ks, hand_vs, sems, taken,
):
    rows, blocks = cache_k.shape[0], hand_k.shape[0]
    copies = [pltpu.make_async_copy(hand_k, hand_ks, sems.at[0]), pltpu.make_async_copy(hand_v, hand_vs, sems.at[1])]
    for row in range(rows):
        copies.append(pltpu.make_async_copy(cache_k.at[row], cache_ks.at[row], sems.at[2 + 2 * row]))
        copies.append(pltpu.make_async_copy(cache_v.at[row], cache_vs.at[row], sems.at[3 + 2 * row]))
    for copy in copies:
        copy.start()
    spread(dec_q, dec_rows)
    spread(hand_q, hand_rows)
    dec_sums[...] = jnp.zeros_like(dec_sums)
    slot_sums[...] = jnp.zeros_like(slot_sums)
    for at in range(taken.shape[0]):
        taken[at] = 0
    copies[0].wait()
    copies[1].wait()
    queries = [hand_rows[pl.ds(at * GROUP, GROUP), :].astype(jnp.bfloat16) for at in range(blocks)]
    s = jnp.concatenate([dot_t(queries[at], hand_ks[at]) for at in range(blocks)], 0) * SCALE
    count = jnp.zeros(s.shape, jnp.int32)
    block_of = lax.broadcasted_iota(jnp.int32, s.shape, 0) // GROUP
    for at in range(blocks):
        count = jnp.where(block_of == at, hand_count[at], count)
    seen = lax.broadcasted_iota(jnp.int32, s.shape, 1) < count
    s, top = softmax_rows(s, seen)
    p = jnp.where(seen, jnp.exp2(s - top), 0.0)
    total = jnp.sum(p, axis=1, keepdims=True)
    summed = [
        dot(p[at * GROUP : (at + 1) * GROUP].astype(jnp.bfloat16), hand_vs[at]) for at in range(blocks)
    ]
    results = jnp.concatenate(summed, 0) / jnp.where(total > 0, total, 1.0)
    for at in range(blocks):
        to = owner[at]
        slot = relative(to, place[0]) * MOST + taken[to]
        taken[to] = taken[to] + 1
        slot_sums[heads_at(slot), :] = results[at * GROUP : (at + 1) * GROUP]
    for copy in copies[2:]:
        copy.wait()
    queries = [dec_rows[pl.ds(row * GROUP, GROUP), :].astype(jnp.bfloat16) for row in range(rows)]
    s = jnp.concatenate([dot_t(queries[row], cache_ks[row]) for row in range(rows)], 0) * SCALE
    keys = jnp.concatenate(
        [jnp.broadcast_to(dec_k[row : row + 1, :].astype(jnp.float32), (GROUP, HEAD_DIM)) for row in range(rows)], 0
    )
    values = jnp.concatenate(
        [jnp.broadcast_to(dec_v[row : row + 1, :].astype(jnp.float32), (GROUP, HEAD_DIM)) for row in range(rows)], 0
    )
    own = jnp.sum(dec_rows[...] * keys, axis=1, keepdims=True) * SCALE
    row_of = lax.broadcasted_iota(jnp.int32, (rows * GROUP, 1), 0) // GROUP
    count = jnp.zeros((rows * GROUP, 1), jnp.int32)
    for row in range(rows):
        count = jnp.where(row_of == row, dec_len[row], count)
    seen = lax.broadcasted_iota(jnp.int32, s.shape, 1) < count
    s, top = softmax_rows(s, seen)
    top = jnp.maximum(top, own)
    p = jnp.where(seen, jnp.exp2(s - top), 0.0)
    own = jnp.exp2(own - top)
    total = jnp.sum(p, axis=1, keepdims=True) + own
    p = p.astype(jnp.bfloat16)
    summed = jnp.concatenate([dot(p[row * GROUP : (row + 1) * GROUP], cache_vs[row]) for row in range(rows)], 0)
    summed = summed + own.astype(jnp.bfloat16).astype(jnp.float32) * values
    dec_sums[pl.ds(0, rows * GROUP), :] = summed / total
    gather_heads(dec_sums, dec_out)
    for step, out in enumerate((slot_0, slot_1, slot_2, slot_3)):
        gather_heads(slot_sums.at[pl.ds(step * 8 * GROUP, 8 * GROUP)], out)


def attend_rows(dec_len, owner, hand_count, place, dec_q, dec_k, dec_v, hand_q, cache_k, cache_v, hand_k, hand_v, owners):
    rows = cache_k.shape[0]
    blocks = hand_k.shape[0]
    width = dec_q.shape[1]
    return pl.pallas_call(
        rows_kernel,
        out_shape=(
            jax.ShapeDtypeStruct((16, width), jnp.bfloat16),
            *[jax.ShapeDtypeStruct((owners * MOST // 4, width), jnp.float32)] * 4,
        ),
        in_specs=[SMEM] * 4
        + [whole(a.shape) for a in (dec_q, dec_k, dec_v, hand_q)]
        + [pl.BlockSpec(memory_space=pl.ANY)] * 4,
        out_specs=(whole((16, width)), *[whole((owners * MOST // 4, width))] * 4),
        scratch_shapes=[
            pltpu.VMEM((rows * GROUP, HEAD_DIM), jnp.float32),
            pltpu.VMEM((blocks * GROUP, HEAD_DIM), jnp.float32),
            pltpu.VMEM((16 * GROUP, HEAD_DIM), jnp.float32),
            pltpu.VMEM((owners * MOST * GROUP, HEAD_DIM), jnp.float32),
            pltpu.VMEM(cache_k.shape, jnp.bfloat16),
            pltpu.VMEM(cache_v.shape, jnp.bfloat16),
            pltpu.VMEM(hand_k.shape, jnp.bfloat16),
            pltpu.VMEM(hand_v.shape, jnp.bfloat16),
            pltpu.SemaphoreType.DMA((2 + 2 * rows,)),
            pltpu.SMEM((owners,), jnp.int32),
        ],
        compiler_params=pltpu.CompilerParams(vmem_limit_bytes=56 * 2**20),
        cost_estimate=pl.CostEstimate(flops=10**6, bytes_accessed=10**4, transcendentals=0),
        name="rows",
    )(dec_len, owner, hand_count, place, dec_q, dec_k, dec_v, hand_q, cache_k, cache_v, hand_k, hand_v)


def part_kernel(count, rows, *refs):
    pieces, (keep, send) = refs[:count], refs[count:]
    at = 0
    for piece in pieces:
        for start in range(0, piece.shape[0], 2 * rows):
            keep[pl.ds(at, rows), :] = piece[pl.ds(start, rows), :]
            send[pl.ds(at, rows), :] = piece[pl.ds(start + rows, rows), :]
            at += rows


def part_rows(pieces, rows, name):
    half = sum(piece.shape[0] for piece in pieces) // 2
    out = jax.ShapeDtypeStruct((half, pieces[0].shape[1]), pieces[0].dtype)
    return pl.pallas_call(
        functools.partial(part_kernel, len(pieces), rows),
        out_shape=(out, out),
        in_specs=[whole(piece.shape) for piece in pieces],
        out_specs=(whole(out.shape),) * 2,
        compiler_params=pltpu.CompilerParams(vmem_limit_bytes=8 * 2**20),
        name=name,
    )(*pieces)


def join_kernel(*refs):
    sources, out, sems = refs[:4], refs[4], refs[5]
    copies = []
    at = 0
    for n, source in enumerate(sources):
        copies.append(pltpu.make_async_copy(source, out.at[pl.ds(at, source.shape[0])], sems.at[n]))
        at += source.shape[0]
    for copy in copies:
        copy.start()
    for copy in copies:
        copy.wait()


def join(*pieces):
    rows = sum(piece.shape[0] for piece in pieces)
    return pl.pallas_call(
        join_kernel,
        out_shape=jax.ShapeDtypeStruct((rows, HEAD_DIM), jnp.bfloat16),
        in_specs=[pl.BlockSpec(memory_space=pl.ANY)] * 4,
        out_specs=whole((rows, HEAD_DIM)),
        scratch_shapes=[pltpu.SemaphoreType.DMA((4,))],
        compiler_params=pltpu.CompilerParams(vmem_limit_bytes=56 * 2**20),
        cost_estimate=pl.CostEstimate(flops=0, bytes_accessed=rows * 512, transcendentals=0),
        name="join",
    )(*pieces)


def column(row):
    return jnp.transpose(jnp.broadcast_to(row, (TOK, TOK)))


def slot_order(place):
    count = 32
    to = lax.broadcasted_iota(jnp.int32, (count, count), 0)
    at = lax.broadcasted_iota(jnp.int32, (count, count), 1)
    core, high, steps, rank = at // 16, (at // 8) % 2, (at // 2) % 4, at % 2
    x = (place // 2 - steps + 4) % 4
    source = ((place // 8) ^ high) * 8 + x * 2 + ((place % 2) ^ core)
    return jnp.where(to == source * 2 + rank, 1.0, 0.0).astype(jnp.bfloat16)


def project_first_kernel(place, order, mine, other, new_a, new_b, dec, weight, *refs):
    outs, attn = refs[:-1], refs[-1]

    @pl.when(pl.program_id(0) == 0)
    def _():
        a_levels, b_levels = unpack_levels(mine), unpack_levels(other)
        top = jnp.maximum(a_levels, b_levels)
        wa, wb = jnp.exp2(a_levels - top), jnp.exp2(b_levels - top)
        wa, wb = wa / (wa + wb), wb / (wa + wb)
        for head in range(GROUP):
            rows = pl.ds(head * TOK, TOK)
            a, b = mine[rows, :].astype(jnp.float32), other[rows, :].astype(jnp.float32)
            mixed = a * column(wa[head : head + 1, :]) + b * column(wb[head : head + 1, :])
            attn[pl.ds(0, TOK), pl.ds(head * HEAD_DIM, HEAD_DIM)] = mixed.astype(attn.dtype)
        new = jnp.concatenate([new_a[...], new_b[...]], 0).astype(jnp.bfloat16)
        attn[pl.ds(TOK, 32), :] = dot(slot_order(place[0]), new).astype(attn.dtype)
        attn[pl.ds(TOK + 32, 16), :] = dec[...]

    project_step(outs, attn, weight)


def project_rest_kernel(order, attn, weight, *outs):
    project_step(outs, attn, weight)


def project_step(outs, attn, weight):
    result = dot(attn[...], weight[...]).astype(jnp.bfloat16)
    for step, out in enumerate(outs):

        @pl.when(pl.program_id(0) == step)
        def _():
            out[...] = result[: out.shape[0]]


def project(kernel, scalars, inputs, weight, rows, attn_shape, vmem, name):
    depth, width = weight.shape
    steps = scalars[-1].shape[0]
    columns = 1024
    outs = [jax.ShapeDtypeStruct((rows, columns), jnp.bfloat16)] * steps
    if attn_shape:
        outs.append(jax.ShapeDtypeStruct(attn_shape, jnp.bfloat16))
    return pl.pallas_call(
        kernel,
        grid_spec=pltpu.PrefetchScalarGridSpec(
            num_scalar_prefetch=len(scalars),
            grid=(steps,),
            in_specs=[whole(a.shape) for a in inputs]
            + [pl.BlockSpec((depth, columns), lambda i, *scalars: (0, scalars[-1][i]))],
            out_specs=[whole(out.shape) for out in outs],
        ),
        out_shape=outs,
        compiler_params=pltpu.CompilerParams(vmem_limit_bytes=vmem),
        cost_estimate=pl.CostEstimate(
            flops=2 * rows * depth * columns * steps, bytes_accessed=2 * depth * columns * steps, transcendentals=0
        ),
        name=name,
    )(*scalars, *inputs, weight)


def total_of(*parts):
    total = parts[0].astype(jnp.float32)
    for part in parts[1:]:
        total = total + part.astype(jnp.float32)
    return total.astype(jnp.bfloat16)


def total_kernel(*refs):
    parts, outs = refs[:-3], refs[-3:]
    total = parts[0][...].astype(jnp.float32)
    for part in parts[1:]:
        total = total + part[...].astype(jnp.float32)
    total = total.astype(jnp.bfloat16)
    at = 0
    for out in outs:
        out[...] = total[at : at + out.shape[0]]
        at += out.shape[0]


def add_up(parts, rows):
    width = parts[0].shape[1]
    return pl.pallas_call(
        total_kernel,
        out_shape=[jax.ShapeDtypeStruct((count, width), jnp.bfloat16) for count in rows],
        in_specs=[whole(part.shape) for part in parts],
        out_specs=[whole((count, width)) for count in rows],
        compiler_params=pltpu.CompilerParams(vmem_limit_bytes=VMEM_LIMIT),
        cost_estimate=pl.CostEstimate(flops=0, bytes_accessed=len(parts) * sum(rows) * width * 2, transcendentals=0),
        name="add_up",
    )(*parts)


def local(
    stretch_start,
    stretch_q,
    stretch_k,
    stretch_v,
    prefix_k,
    prefix_v,
    dec_len,
    dec_q,
    dec_k,
    dec_v,
    cache_k,
    cache_v,
    hand_owner,
    hand_count,
    hand_q,
    hand_k,
    hand_v,
    out_weight,
):
    place = lax.axis_index("ctx")
    me = lax.axis_index("tp")
    y, x, c = place // 8, (place // 2) % 4, place % 2

    b0 = join(prefix_k, stretch_k, prefix_v, stretch_v)
    b1 = lax.ppermute(b0, "ctx", X_UP)
    b2 = lax.ppermute(b0, "ctx", X_DOWN)
    c0 = lax.ppermute(b0, "ctx", CORE_SWAP)
    other_q = lax.ppermute(stretch_q, "ctx", Y_SWAP)
    up, down, two = (x + 1) % 4, (x + 3) % 4, (x + 2) % 4
    info = jnp.stack(
        [
            stretch_start[0],
            place,
            ctx_index(1 - y, x, c),
            place,
            ctx_index(y, x, 1 - c),
            ctx_index(y, down, c),
            ctx_index(y, down, 1 - c),
            ctx_index(y, up, c),
            ctx_index(y, up, 1 - c),
            ctx_index(y, two, c),
            ctx_index(y, two, 1 - c),
        ]
    ).astype(jnp.int32)

    h, z = me // 4, me % 4
    order_far = jnp.stack([tp_index(1 - h, z + 1), tp_index(1 - h, z + 3), tp_index(1 - h, z + 2)]).astype(jnp.int32)
    order_near = jnp.stack(
        [tp_index(h, z + 1), tp_index(h, z + 3), tp_index(1 - h, z), tp_index(h, z + 2), me]
    ).astype(jnp.int32)
    orders = (order_far, order_near)
    ctx_count = lax.axis_size("ctx")
    at_place = place[None].astype(jnp.int32)
    info, orders, at_place = lax.optimization_barrier((info, orders, at_place))
    dec_attn, *slots = attend_rows(
        dec_len, hand_owner[:, 0], hand_count, at_place, dec_q, dec_k, dec_v, hand_q,
        cache_k, cache_v, hand_k, hand_v, ctx_count,
    )
    info, orders, other_q, dec_attn = lax.optimization_barrier((info, orders, other_q, dec_attn))
    own = attend(info, [stretch_q], (0,), 0, [b0, c0], [], "attend_own")
    info, b0_later, b1, b2, own = lax.optimization_barrier((info, b0, b1, b2, own))
    b4 = lax.ppermute(b0_later, "ctx", X_TWO)
    c1 = lax.ppermute(b1, "ctx", CORE_SWAP)
    c2 = lax.ppermute(b2, "ctx", CORE_SWAP)
    theirs = attend(info, [other_q], (1,), 0, [b0, c0], [], "attend_other")

    state = attend(info, [stretch_q, other_q], (0, 1), 2, [b1, c1, b2, c2], own + theirs, "attend_both")

    slots, state, b4 = lax.optimization_barrier((slots, state, b4))
    c4 = lax.ppermute(b4, "ctx", CORE_SWAP)
    slots[1] = lax.ppermute(slots[1], "ctx", X_UP)
    slots[2] = lax.ppermute(slots[2], "ctx", X_TWO)
    slots[3] = lax.ppermute(slots[3], "ctx", X_DOWN)
    before = [b0, c0, b1, c1, b2, c2]
    give = attend_last(info, other_q, 1, before, [b4, c4], state[2:], "attend_give")
    slots, give = lax.optimization_barrier((slots, give))
    other = lax.ppermute(give, "ctx", Y_SWAP)
    keep, send = part_rows(slots, 4, "part_y")
    got = lax.ppermute(send, "ctx", Y_SWAP)
    mine = attend_last(info, stretch_q, 0, before, [b4, c4], state[:2], "attend_keep")
    keep, got, mine = lax.optimization_barrier((keep, got, mine))
    new_a, send = part_rows([keep, got], 2, "part_core")
    new_b = lax.ppermute(send, "ctx", CORE_SWAP)

    counts = (TOK, ctx_count * MOST, dec_q.shape[0])
    rows = sum(counts)
    above_far, below_far, cross, attn = project(
        project_first_kernel, (at_place, orders[0]), (mine, other, new_a, new_b, dec_attn), out_weight, rows,
        (TOK + 32 + 16, out_weight.shape[0]), VMEM_LIMIT, "project_far",
    )
    above_far = lax.ppermute(above_far, "tp", Z_UP)
    below_far = lax.ppermute(below_far, "tp", Z_DOWN)
    cross = lax.ppermute(cross, "tp", H_SWAP)
    above, below, across, two, own = project(
        project_rest_kernel, (orders[1],), (attn,), out_weight, rows, None, VMEM_LIMIT, "project_near"
    )
    above, below, above_far, below_far = lax.optimization_barrier((above, below, above_far, below_far))
    above = lax.ppermute(above, "tp", Z_UP)
    below = lax.ppermute(below, "tp", Z_DOWN)
    across = lax.ppermute(total_of(across, above_far, below_far), "tp", H_SWAP)
    two = lax.ppermute(total_of(two, cross), "tp", Z_TWO)
    stretch_out, new_out, dec_out = add_up([own, above, below, two, across], counts)
    return stretch_out, dec_out, new_out


def solution(mesh):
    in_specs = (
        P(),
        P("ctx", "tp"),
        P("ctx", "tp"),
        P("ctx", "tp"),
        P("ctx", "tp"),
        P("ctx", "tp"),
        P("ctx"),
        P("ctx", "tp"),
        P("ctx", "tp"),
        P("ctx", "tp"),
        P("ctx", None, "tp"),
        P("ctx", None, "tp"),
        P("ctx", None),
        P("ctx"),
        P("ctx", "tp"),
        P("ctx", None, "tp"),
        P("ctx", None, "tp"),
        P("tp", None),
    )
    out_specs = (P("ctx", "tp"), P("ctx", "tp"), P("ctx", "tp"))
    return jax.shard_map(local, mesh=mesh, in_specs=in_specs, out_specs=out_specs, check_vma=False)
```

```python
import functools
import math

import jax
import jax.numpy as jnp
from jax import lax
from jax.experimental import pallas as pl
from jax.experimental.pallas import tpu as pltpu
from jax.sharding import PartitionSpec as P

HEAD_DIM = 128
MOST = 2
GROUP = 8
TOK = 128
PRE = 1024
BLOCK = PRE + TOK
ROWS = GROUP * TOK
TILE = 512
SUB = 256
NEG = -1e30
SCALE = math.log2(math.e) / math.sqrt(HEAD_DIM)
LOW, HIGH = 2.0**-60, 2.0**100
VMEM_LIMIT = 24 * 2**20
STATS = 32


def dot_t(a, b):
    return lax.dot_general(a, b, (((1,), (1,)), ((), ())), preferred_element_type=jnp.float32)


def dot(a, b):
    return jnp.dot(a, b, preferred_element_type=jnp.float32)


def ctx_index(y, x, c):
    return y * 8 + x * 2 + c


def ctx_perm(move):
    return [
        (ctx_index(y, x, c), ctx_index(*move(y, x, c)))
        for y in range(2)
        for x in range(4)
        for c in range(2)
    ]


X_UP = ctx_perm(lambda y, x, c: (y, (x + 1) % 4, c))
X_DOWN = ctx_perm(lambda y, x, c: (y, (x + 3) % 4, c))
X_TWO = ctx_perm(lambda y, x, c: (y, (x + 2) % 4, c))
Y_SWAP = ctx_perm(lambda y, x, c: (1 - y, x, c))
CORE_SWAP = ctx_perm(lambda y, x, c: (y, x, 1 - c))


def tp_index(h, z):
    return h * 4 + z % 4


def tp_perm(move):
    return [(tp_index(h, z), tp_index(*move(h, z))) for h in range(2) for z in range(4)]


Z_UP = tp_perm(lambda h, z: (h, z + 1))
Z_DOWN = tp_perm(lambda h, z: (h, z + 3))
Z_TWO = tp_perm(lambda h, z: (h, z + 2))
H_SWAP = tp_perm(lambda h, z: (1 - h, z))


def lane_sums(p):
    total = p[:, 0:128]
    for at in range(128, p.shape[1], 128):
        total = total + p[:, at : at + 128]
    return total


def stack_queries(q_refs, queries):
    for half, ref in enumerate(q_refs):
        for head in range(GROUP):
            queries[pl.ds(half * ROWS + head * TOK, TOK), :] = ref[:, pl.ds(head * HEAD_DIM, HEAD_DIM)]


def add_block(info, block_at, kv, queries, acc, sums, halves):
    prefix_end = info[0]
    chunk = info[3 + block_at]
    count = jnp.clip(prefix_end - chunk * PRE, 0, PRE)

    @pl.when(count == PRE)
    def _():
        for tile in range(len(halves) * ROWS // TILE):
            rows = pl.ds(tile * TILE, TILE)
            for at in range(0, PRE, 512):
                p = jnp.exp2(dot_t(queries[rows, :], kv[pl.ds(at, 512), :]) * SCALE)
                acc[rows, :] += dot(p.astype(jnp.bfloat16), kv[pl.ds(BLOCK + at, 512), :])
                sums[rows, :] += lane_sums(p)

    @pl.when(jnp.logical_and(count > 0, count < PRE))
    def _():
        def step(at, carry):
            start = pl.multiple_of(at * SUB, SUB)
            columns = start + lax.broadcasted_iota(jnp.int32, (TILE, SUB), 1)
            for tile in range(len(halves) * ROWS // TILE):
                rows = pl.ds(tile * TILE, TILE)
                s = dot_t(queries[rows, :], kv[pl.ds(start, SUB), :]) * SCALE
                p = jnp.where(columns < count, jnp.exp2(s), 0.0)
                acc[rows, :] += dot(p.astype(jnp.bfloat16), kv[pl.ds(BLOCK + start, SUB), :])
                sums[rows, :] += lane_sums(p)
            return carry

        lax.fori_loop(0, (count + SUB - 1) // SUB, step, 0)


def add_tokens(info, first_block, kvs, queries, acc, sums, halves, near):
    count = len(kvs)
    width = count * TOK
    for at, kv in enumerate(kvs):
        near[pl.ds(at * TOK, TOK), :] = kv[pl.ds(PRE, TOK), :]
        near[pl.ds(width + at * TOK, TOK), :] = kv[pl.ds(BLOCK + PRE, TOK), :]
    for at_half, half in enumerate(halves):
        place = info[1 + half]
        seen_from = [place - info[3 + first_block + at] for at in range(count)]
        some = functools.reduce(jnp.maximum, seen_from)

        @pl.when(some >= 0)
        def _():
            column = lax.broadcasted_iota(jnp.int32, (1, width), 1)
            start = jnp.zeros((1, width), jnp.int32)
            for at in range(count):
                least = jnp.where(seen_from[at] > 0, -TOK, jnp.where(seen_from[at] == 0, 0, TOK))
                start = jnp.where(column // TOK == at, least, start)
            start = start + column % TOK
            token = lax.broadcasted_iota(jnp.int32, (TILE, width), 0) % TOK
            seen = start <= token
            for tile in range(ROWS // TILE):
                rows = pl.ds(at_half * ROWS + tile * TILE, TILE)
                s = dot_t(queries[rows, :], near[pl.ds(0, width), :]) * SCALE
                p = jnp.where(seen, jnp.exp2(s), 0.0)
                acc[rows, :] += dot(p.astype(jnp.bfloat16), near[pl.ds(width, width), :])
                sums[rows, :] += lane_sums(p)


def shifted_step(rows, s, seen, values, queries, acc, sums, peak):
    s = jnp.where(seen, s, NEG)
    before = peak[rows, :]
    now = jnp.maximum(before, jnp.max(s, axis=1, keepdims=True))
    p = jnp.where(seen, jnp.exp2(s - now[:, 0:1]), 0.0)
    fade = jnp.exp2(before - now)
    acc[rows, :] = acc[rows, :] * fade + dot(p.astype(jnp.bfloat16), values)
    sums[rows, :] = sums[rows, :] * fade + lane_sums(p)
    peak[rows, :] = now


def shifted_block(info, chunk, place, kv, queries, acc, sums, peak):
    count = jnp.clip(info[0] - chunk * PRE, 0, PRE)
    tile_rows = 256

    def tile_step(tile, carry):
        rows = pl.ds(pl.multiple_of(tile * tile_rows, tile_rows), tile_rows)

        def step(at, carry):
            start = pl.multiple_of(at * SUB, SUB)
            columns = start + lax.broadcasted_iota(jnp.int32, (tile_rows, SUB), 1)
            s = dot_t(queries[rows, :], kv[pl.ds(start, SUB), :]) * SCALE
            shifted_step(rows, s, columns < count, kv[pl.ds(BLOCK + start, SUB), :], queries, acc, sums, peak)
            return carry

        lax.fori_loop(0, (count + SUB - 1) // SUB, step, 0)

        @pl.when(chunk <= place)
        def _():
            token = lax.broadcasted_iota(jnp.int32, (tile_rows, TOK), 0) % TOK
            key = lax.broadcasted_iota(jnp.int32, (tile_rows, TOK), 1)
            seen = key <= token + jnp.where(chunk < place, TOK, 0)
            s = dot_t(queries[rows, :], kv[pl.ds(PRE, TOK), :]) * SCALE
            shifted_step(rows, s, seen, kv[pl.ds(BLOCK + PRE, TOK), :], queries, acc, sums, peak)

        return carry

    lax.fori_loop(0, ROWS // tile_rows, tile_step, 0)


def attend_kernel(halves, first_block, blocks, starts, info, *refs):
    count = len(halves)
    q_refs, refs = refs[:count], refs[count:]
    kvs, refs = refs[:blocks], refs[blocks:]
    if not starts:
        before, refs = refs[: 2 * count], refs[2 * count :]
    after, (queries, acc, sums, near) = refs[: 2 * count], refs[2 * count :]
    stack_queries(q_refs, queries)
    if starts:
        acc[...] = jnp.zeros_like(acc)
        sums[...] = jnp.zeros_like(sums)
    else:
        for at in range(count):
            acc[pl.ds(at * ROWS, ROWS), :] = before[2 * at][...]
            sums[pl.ds(at * ROWS, ROWS), :] = before[2 * at + 1][...]
    for at in range(blocks):
        add_block(info, first_block + at, kvs[at], queries, acc, sums, halves)
    add_tokens(info, first_block, kvs, queries, acc, sums, halves, near)
    for at in range(count):
        after[2 * at][...] = acc[pl.ds(at * ROWS, ROWS), :]
        after[2 * at + 1][...] = sums[pl.ds(at * ROWS, ROWS), :]


def last_kernel(half, earlier, blocks, info, q_ref, *refs):
    earlier_kvs, refs = refs[:earlier], refs[earlier:]
    kvs, refs = refs[:blocks], refs[blocks:]
    acc_in, sums_in, out, queries, acc, sums, near, peak, held, levels, sem = refs
    stack_queries((q_ref,), queries)
    acc[...] = acc_in[...]
    sums[...] = sums_in[...]
    for at in range(blocks):
        add_block(info, earlier + at, kvs[at], queries, acc, sums, (half,))
    add_tokens(info, earlier, kvs, queries, acc, sums, (half,), near)
    peak[...] = jnp.zeros_like(peak)
    has_keys = jnp.int32(0)
    for at in range(earlier + blocks):
        chunk = info[3 + at]
        some = jnp.logical_or(info[0] > chunk * PRE, chunk <= info[1 + half])
        has_keys = jnp.where(some, 1, has_keys)
    total = jnp.sum(sums[...], axis=1, keepdims=True)
    inside = jnp.where(jnp.logical_and(total >= LOW, total <= HIGH), 1.0, 0.0)

    @pl.when(jnp.logical_and(has_keys > 0, jnp.min(inside) < 0.5))
    def _():
        acc[...] = jnp.zeros_like(acc)
        sums[...] = jnp.zeros_like(sums)
        peak[...] = jnp.full_like(peak, NEG)

        def block_step(at, carry):
            for one in range(earlier + blocks):
                source = earlier_kvs[one] if one < earlier else kvs[one - earlier]

                @pl.when(at == one)
                def _():
                    copy = pltpu.make_async_copy(source, held, sem)
                    copy.start()
                    copy.wait()

            shifted_block(info, info[3 + at], info[1 + half], held, queries, acc, sums, peak)
            return carry

        lax.fori_loop(0, earlier + blocks, block_step, 0)

    for head in range(GROUP):
        rows = pl.ds(head * TOK, TOK)
        total = jnp.sum(sums[rows, :], axis=1, keepdims=True)
        out[rows, :] = (acc[rows, :] / jnp.where(total > 0, total, 1.0)).astype(out.dtype)
        level = jnp.where(total > 0, peak[rows, :] + jnp.log2(jnp.where(total > 0, total, 1.0)), NEG)
        levels[pl.ds(head, 1), :] = jnp.transpose(level)[0:1, :]
    high = levels[...].astype(jnp.bfloat16)
    rest = levels[...] - high.astype(jnp.float32)
    middle = rest.astype(jnp.bfloat16)
    low = (rest - middle.astype(jnp.float32)).astype(jnp.bfloat16)
    out[pl.ds(ROWS, STATS), :] = jnp.concatenate([high, middle, low, jnp.zeros_like(low)], 0)


def unpack_levels(packed):
    pieces = [packed[pl.ds(ROWS, STATS), :].astype(jnp.float32)]
    return pieces[0][0:8] + pieces[0][8:16] + pieces[0][16:24]


def whole(shape):
    return pl.BlockSpec(shape, lambda *_: (0,) * len(shape))


SMEM = pl.BlockSpec(memory_space=pltpu.SMEM)
STATE = jax.ShapeDtypeStruct((ROWS, 128), jnp.float32)


def attend_cost(halves, blocks):
    return pl.CostEstimate(
        flops=blocks * 4 * halves * ROWS * BLOCK * HEAD_DIM * 2,
        bytes_accessed=blocks * BLOCK * 512 + 4 * halves * ROWS * 512,
        transcendentals=blocks * halves * ROWS * BLOCK,
    )


def attend(info, queries, halves, first_block, kvs, state, name):
    blocks, count = len(kvs), len(halves)
    return pl.pallas_call(
        functools.partial(attend_kernel, halves, first_block, blocks, not state),
        out_shape=[STATE] * (2 * count),
        in_specs=[SMEM]
        + [whole(q.shape) for q in queries]
        + [whole(kv.shape) for kv in kvs]
        + [whole(STATE.shape)] * len(state),
        out_specs=[whole(STATE.shape)] * (2 * count),
        scratch_shapes=[
            pltpu.VMEM((count * ROWS, HEAD_DIM), jnp.bfloat16),
            pltpu.VMEM((count * ROWS, 128), jnp.float32),
            pltpu.VMEM((count * ROWS, 128), jnp.float32),
            pltpu.VMEM((2 * blocks * TOK, HEAD_DIM), jnp.bfloat16),
        ],
        compiler_params=pltpu.CompilerParams(vmem_limit_bytes=VMEM_LIMIT),
        cost_estimate=attend_cost(count, blocks),
        name=name,
    )(info, *queries, *kvs, *state)


def attend_last(info, q, half, earlier, kvs, state, name):
    blocks = len(kvs)
    packed = jax.ShapeDtypeStruct((ROWS + STATS, HEAD_DIM), jnp.bfloat16)
    return pl.pallas_call(
        functools.partial(last_kernel, half, len(earlier), blocks),
        grid=(1,),
        out_shape=packed,
        in_specs=[SMEM, whole(q.shape)]
        + [pl.BlockSpec(memory_space=pl.ANY)] * len(earlier)
        + [whole(kv.shape) for kv in kvs]
        + [whole(STATE.shape)] * 2,
        out_specs=whole(packed.shape),
        scratch_shapes=[
            pltpu.VMEM((ROWS, HEAD_DIM), jnp.bfloat16),
            pltpu.VMEM((ROWS, 128), jnp.float32),
            pltpu.VMEM((ROWS, 128), jnp.float32),
            pltpu.VMEM((2 * blocks * TOK, HEAD_DIM), jnp.bfloat16),
            pltpu.VMEM((ROWS, 128), jnp.float32),
            pltpu.VMEM((2 * BLOCK, HEAD_DIM), jnp.bfloat16),
            pltpu.VMEM((GROUP, TOK), jnp.float32),
            pltpu.SemaphoreType.DMA(()),
        ],
        compiler_params=pltpu.CompilerParams(vmem_limit_bytes=VMEM_LIMIT),
        cost_estimate=attend_cost(1, blocks),
        name=name,
    )(info, q, *earlier, *kvs, *state)


def softmax_rows(s, seen):
    s = jnp.where(seen, s, NEG)
    return s, jnp.max(s, axis=1, keepdims=True)


def spread(rows, flat):
    for head in range(GROUP):
        piece = rows[:, pl.ds(head * HEAD_DIM, HEAD_DIM)].astype(jnp.float32)
        flat[pl.ds(head, rows.shape[0], stride=GROUP), :] = piece


def gather_heads(flat, rows):
    for head in range(GROUP):
        piece = flat[pl.ds(head, rows.shape[0], stride=GROUP), :]
        rows[:, pl.ds(head * HEAD_DIM, HEAD_DIM)] = piece.astype(rows.dtype)


def heads_at(row):
    return pl.ds(pl.multiple_of(row * GROUP, GROUP), GROUP)


def relative(to, place):
    x_steps = (to // 2 - place // 2 + 4) % 4
    return x_steps * 4 + ((to // 8) ^ (place // 8)) * 2 + ((to % 2) ^ (place % 2))


def rows_kernel(
    dec_len, owner, hand_count, place, dec_q, dec_k, dec_v, hand_q, cache_k, cache_v, hand_k, hand_v,
    dec_out, slot_0, slot_1, slot_2, slot_3,
    dec_rows, hand_rows, dec_sums, slot_sums, cache_ks, cache_vs, hand_ks, hand_vs, sems, taken,
):
    rows, blocks = cache_k.shape[0], hand_k.shape[0]
    copies = [pltpu.make_async_copy(hand_k, hand_ks, sems.at[0]), pltpu.make_async_copy(hand_v, hand_vs, sems.at[1])]
    for row in range(rows):
        copies.append(pltpu.make_async_copy(cache_k.at[row], cache_ks.at[row], sems.at[2 + 2 * row]))
        copies.append(pltpu.make_async_copy(cache_v.at[row], cache_vs.at[row], sems.at[3 + 2 * row]))
    for copy in copies:
        copy.start()
    spread(dec_q, dec_rows)
    spread(hand_q, hand_rows)
    dec_sums[...] = jnp.zeros_like(dec_sums)
    slot_sums[...] = jnp.zeros_like(slot_sums)
    for at in range(taken.shape[0]):
        taken[at] = 0
    copies[0].wait()
    copies[1].wait()
    queries = [hand_rows[pl.ds(at * GROUP, GROUP), :].astype(jnp.bfloat16) for at in range(blocks)]
    s = jnp.concatenate([dot_t(queries[at], hand_ks[at]) for at in range(blocks)], 0) * SCALE
    count = jnp.zeros(s.shape, jnp.int32)
    block_of = lax.broadcasted_iota(jnp.int32, s.shape, 0) // GROUP
    for at in range(blocks):
        count = jnp.where(block_of == at, hand_count[at], count)
    seen = lax.broadcasted_iota(jnp.int32, s.shape, 1) < count
    s, top = softmax_rows(s, seen)
    p = jnp.where(seen, jnp.exp2(s - top), 0.0)
    total = jnp.sum(p, axis=1, keepdims=True)
    summed = [
        dot(p[at * GROUP : (at + 1) * GROUP].astype(jnp.bfloat16), hand_vs[at]) for at in range(blocks)
    ]
    results = jnp.concatenate(summed, 0) / jnp.where(total > 0, total, 1.0)
    for at in range(blocks):
        to = owner[at]
        slot = relative(to, place[0]) * MOST + taken[to]
        taken[to] = taken[to] + 1
        slot_sums[heads_at(slot), :] = results[at * GROUP : (at + 1) * GROUP]
    for copy in copies[2:]:
        copy.wait()
    queries = [dec_rows[pl.ds(row * GROUP, GROUP), :].astype(jnp.bfloat16) for row in range(rows)]
    s = jnp.concatenate([dot_t(queries[row], cache_ks[row]) for row in range(rows)], 0) * SCALE
    keys = jnp.concatenate(
        [jnp.broadcast_to(dec_k[row : row + 1, :].astype(jnp.float32), (GROUP, HEAD_DIM)) for row in range(rows)], 0
    )
    values = jnp.concatenate(
        [jnp.broadcast_to(dec_v[row : row + 1, :].astype(jnp.float32), (GROUP, HEAD_DIM)) for row in range(rows)], 0
    )
    own = jnp.sum(dec_rows[...] * keys, axis=1, keepdims=True) * SCALE
    row_of = lax.broadcasted_iota(jnp.int32, (rows * GROUP, 1), 0) // GROUP
    count = jnp.zeros((rows * GROUP, 1), jnp.int32)
    for row in range(rows):
        count = jnp.where(row_of == row, dec_len[row], count)
    seen = lax.broadcasted_iota(jnp.int32, s.shape, 1) < count
    s, top = softmax_rows(s, seen)
    top = jnp.maximum(top, own)
    p = jnp.where(seen, jnp.exp2(s - top), 0.0)
    own = jnp.exp2(own - top)
    total = jnp.sum(p, axis=1, keepdims=True) + own
    p = p.astype(jnp.bfloat16)
    summed = jnp.concatenate([dot(p[row * GROUP : (row + 1) * GROUP], cache_vs[row]) for row in range(rows)], 0)
    summed = summed + own.astype(jnp.bfloat16).astype(jnp.float32) * values
    dec_sums[pl.ds(0, rows * GROUP), :] = summed / total
    gather_heads(dec_sums, dec_out)
    for step, out in enumerate((slot_0, slot_1, slot_2, slot_3)):
        gather_heads(slot_sums.at[pl.ds(step * 8 * GROUP, 8 * GROUP)], out)


def attend_rows(dec_len, owner, hand_count, place, dec_q, dec_k, dec_v, hand_q, cache_k, cache_v, hand_k, hand_v, owners):
    rows = cache_k.shape[0]
    blocks = hand_k.shape[0]
    width = dec_q.shape[1]
    return pl.pallas_call(
        rows_kernel,
        out_shape=(
            jax.ShapeDtypeStruct((16, width), jnp.bfloat16),
            *[jax.ShapeDtypeStruct((owners * MOST // 4, width), jnp.float32)] * 4,
        ),
        in_specs=[SMEM] * 4
        + [whole(a.shape) for a in (dec_q, dec_k, dec_v, hand_q)]
        + [pl.BlockSpec(memory_space=pl.ANY)] * 4,
        out_specs=(whole((16, width)), *[whole((owners * MOST // 4, width))] * 4),
        scratch_shapes=[
            pltpu.VMEM((rows * GROUP, HEAD_DIM), jnp.float32),
            pltpu.VMEM((blocks * GROUP, HEAD_DIM), jnp.float32),
            pltpu.VMEM((16 * GROUP, HEAD_DIM), jnp.float32),
            pltpu.VMEM((owners * MOST * GROUP, HEAD_DIM), jnp.float32),
            pltpu.VMEM(cache_k.shape, jnp.bfloat16),
            pltpu.VMEM(cache_v.shape, jnp.bfloat16),
            pltpu.VMEM(hand_k.shape, jnp.bfloat16),
            pltpu.VMEM(hand_v.shape, jnp.bfloat16),
            pltpu.SemaphoreType.DMA((2 + 2 * rows,)),
            pltpu.SMEM((owners,), jnp.int32),
        ],
        compiler_params=pltpu.CompilerParams(vmem_limit_bytes=56 * 2**20),
        cost_estimate=pl.CostEstimate(flops=10**6, bytes_accessed=10**4, transcendentals=0),
        name="rows",
    )(dec_len, owner, hand_count, place, dec_q, dec_k, dec_v, hand_q, cache_k, cache_v, hand_k, hand_v)


def part_kernel(count, rows, *refs):
    pieces, (keep, send) = refs[:count], refs[count:]
    at = 0
    for piece in pieces:
        for start in range(0, piece.shape[0], 2 * rows):
            keep[pl.ds(at, rows), :] = piece[pl.ds(start, rows), :]
            send[pl.ds(at, rows), :] = piece[pl.ds(start + rows, rows), :]
            at += rows


def part_rows(pieces, rows, name):
    half = sum(piece.shape[0] for piece in pieces) // 2
    out = jax.ShapeDtypeStruct((half, pieces[0].shape[1]), pieces[0].dtype)
    return pl.pallas_call(
        functools.partial(part_kernel, len(pieces), rows),
        out_shape=(out, out),
        in_specs=[whole(piece.shape) for piece in pieces],
        out_specs=(whole(out.shape),) * 2,
        compiler_params=pltpu.CompilerParams(vmem_limit_bytes=8 * 2**20),
        name=name,
    )(*pieces)


def join_kernel(*refs):
    sources, out, sems = refs[:4], refs[4], refs[5]
    copies = []
    at = 0
    for n, source in enumerate(sources):
        copies.append(pltpu.make_async_copy(source, out.at[pl.ds(at, source.shape[0])], sems.at[n]))
        at += source.shape[0]
    for copy in copies:
        copy.start()
    for copy in copies:
        copy.wait()


def join(*pieces):
    rows = sum(piece.shape[0] for piece in pieces)
    return pl.pallas_call(
        join_kernel,
        out_shape=jax.ShapeDtypeStruct((rows, HEAD_DIM), jnp.bfloat16),
        in_specs=[pl.BlockSpec(memory_space=pl.ANY)] * 4,
        out_specs=whole((rows, HEAD_DIM)),
        scratch_shapes=[pltpu.SemaphoreType.DMA((4,))],
        compiler_params=pltpu.CompilerParams(vmem_limit_bytes=56 * 2**20),
        cost_estimate=pl.CostEstimate(flops=0, bytes_accessed=rows * 512, transcendentals=0),
        name="join",
    )(*pieces)


def column(row):
    return jnp.transpose(jnp.broadcast_to(row, (TOK, TOK)))


def slot_order(place):
    count = 32
    to = lax.broadcasted_iota(jnp.int32, (count, count), 0)
    at = lax.broadcasted_iota(jnp.int32, (count, count), 1)
    core, high, steps, rank = at // 16, (at // 8) % 2, (at // 2) % 4, at % 2
    x = (place // 2 - steps + 4) % 4
    source = ((place // 8) ^ high) * 8 + x * 2 + ((place % 2) ^ core)
    return jnp.where(to == source * 2 + rank, 1.0, 0.0).astype(jnp.bfloat16)


def project_first_kernel(place, order, mine, other, new_a, new_b, dec, weight, *refs):
    outs, attn = refs[:-1], refs[-1]

    @pl.when(pl.program_id(0) == 0)
    def _():
        a_levels, b_levels = unpack_levels(mine), unpack_levels(other)
        top = jnp.maximum(a_levels, b_levels)
        wa, wb = jnp.exp2(a_levels - top), jnp.exp2(b_levels - top)
        wa, wb = wa / (wa + wb), wb / (wa + wb)
        for head in range(GROUP):
            rows = pl.ds(head * TOK, TOK)
            a, b = mine[rows, :].astype(jnp.float32), other[rows, :].astype(jnp.float32)
            mixed = a * column(wa[head : head + 1, :]) + b * column(wb[head : head + 1, :])
            attn[pl.ds(0, TOK), pl.ds(head * HEAD_DIM, HEAD_DIM)] = mixed.astype(attn.dtype)
        new = jnp.concatenate([new_a[...], new_b[...]], 0).astype(jnp.bfloat16)
        attn[pl.ds(TOK, 32), :] = dot(slot_order(place[0]), new).astype(attn.dtype)
        attn[pl.ds(TOK + 32, 16), :] = dec[...]

    project_step(outs, attn, weight)


def project_rest_kernel(order, attn, weight, *outs):
    project_step(outs, attn, weight)


def project_step(outs, attn, weight):
    result = dot(attn[...], weight[...]).astype(jnp.bfloat16)
    for step, out in enumerate(outs):

        @pl.when(pl.program_id(0) == step)
        def _():
            out[...] = result[: out.shape[0]]


def project(kernel, scalars, inputs, weight, rows, attn_shape, vmem, name):
    depth, width = weight.shape
    steps = scalars[-1].shape[0]
    columns = 1024
    outs = [jax.ShapeDtypeStruct((rows, columns), jnp.bfloat16)] * steps
    if attn_shape:
        outs.append(jax.ShapeDtypeStruct(attn_shape, jnp.bfloat16))
    return pl.pallas_call(
        kernel,
        grid_spec=pltpu.PrefetchScalarGridSpec(
            num_scalar_prefetch=len(scalars),
            grid=(steps,),
            in_specs=[whole(a.shape) for a in inputs]
            + [pl.BlockSpec((depth, columns), lambda i, *scalars: (0, scalars[-1][i]))],
            out_specs=[whole(out.shape) for out in outs],
        ),
        out_shape=outs,
        compiler_params=pltpu.CompilerParams(vmem_limit_bytes=vmem),
        cost_estimate=pl.CostEstimate(
            flops=2 * rows * depth * columns * steps, bytes_accessed=2 * depth * columns * steps, transcendentals=0
        ),
        name=name,
    )(*scalars, *inputs, weight)


def total_of(*parts):
    total = parts[0].astype(jnp.float32)
    for part in parts[1:]:
        total = total + part.astype(jnp.float32)
    return total.astype(jnp.bfloat16)


def total_kernel(count, *refs):
    parts, outs = refs[:count], refs[count:]
    total = parts[0][...].astype(jnp.float32)
    for part in parts[1:]:
        total = total + part[...].astype(jnp.float32)
    total = total.astype(jnp.bfloat16)
    at = 0
    for out in outs:
        out[...] = total[at : at + out.shape[0]]
        at += out.shape[0]


def add_up(parts, rows, name, flops):
    width = parts[0].shape[1]
    return pl.pallas_call(
        functools.partial(total_kernel, len(parts)),
        out_shape=[jax.ShapeDtypeStruct((count, width), jnp.bfloat16) for count in rows],
        in_specs=[whole(part.shape) for part in parts],
        out_specs=[whole((count, width)) for count in rows],
        compiler_params=pltpu.CompilerParams(vmem_limit_bytes=VMEM_LIMIT),
        cost_estimate=pl.CostEstimate(flops=flops, bytes_accessed=len(parts) * sum(rows) * width * 2, transcendentals=0),
        name=name,
    )(*parts)


def local(
    stretch_start,
    stretch_q,
    stretch_k,
    stretch_v,
    prefix_k,
    prefix_v,
    dec_len,
    dec_q,
    dec_k,
    dec_v,
    cache_k,
    cache_v,
    hand_owner,
    hand_count,
    hand_q,
    hand_k,
    hand_v,
    out_weight,
):
    place = lax.axis_index("ctx")
    me = lax.axis_index("tp")
    y, x, c = place // 8, (place // 2) % 4, place % 2

    b0 = join(prefix_k, stretch_k, prefix_v, stretch_v)
    b1 = lax.ppermute(b0, "ctx", X_UP)
    b2 = lax.ppermute(b0, "ctx", X_DOWN)
    c0 = lax.ppermute(b0, "ctx", CORE_SWAP)
    other_q = lax.ppermute(stretch_q, "ctx", Y_SWAP)
    up, down, two = (x + 1) % 4, (x + 3) % 4, (x + 2) % 4
    info = jnp.stack(
        [
            stretch_start[0],
            place,
            ctx_index(1 - y, x, c),
            place,
            ctx_index(y, x, 1 - c),
            ctx_index(y, down, c),
            ctx_index(y, down, 1 - c),
            ctx_index(y, up, c),
            ctx_index(y, up, 1 - c),
            ctx_index(y, two, c),
            ctx_index(y, two, 1 - c),
        ]
    ).astype(jnp.int32)

    h, z = me // 4, me % 4
    order_far = jnp.stack([tp_index(1 - h, z + 1), tp_index(1 - h, z + 3), tp_index(1 - h, z + 2)]).astype(jnp.int32)
    order_near = jnp.stack(
        [tp_index(h, z + 1), tp_index(h, z + 3), tp_index(1 - h, z), tp_index(h, z + 2), me]
    ).astype(jnp.int32)
    orders = (order_far, order_near)
    ctx_count = lax.axis_size("ctx")
    at_place = place[None].astype(jnp.int32)
    info, orders, at_place = lax.optimization_barrier((info, orders, at_place))
    dec_attn, *slots = attend_rows(
        dec_len, hand_owner[:, 0], hand_count, at_place, dec_q, dec_k, dec_v, hand_q,
        cache_k, cache_v, hand_k, hand_v, ctx_count,
    )
    info, orders, other_q, dec_attn = lax.optimization_barrier((info, orders, other_q, dec_attn))
    state = attend(info, [stretch_q, other_q], (0, 1), 0, [b0, c0], [], "attend_first")
    info, b0_later, b1, b2, state = lax.optimization_barrier((info, b0, b1, b2, state))
    b4 = lax.ppermute(b0_later, "ctx", X_TWO)
    c1 = lax.ppermute(b1, "ctx", CORE_SWAP)
    c2 = lax.ppermute(b2, "ctx", CORE_SWAP)

    state = attend(info, [stretch_q, other_q], (0, 1), 2, [b1, c1, b2, c2], state, "attend_both")

    slots, state, b4 = lax.optimization_barrier((slots, state, b4))
    c4 = lax.ppermute(b4, "ctx", CORE_SWAP)
    slots[1] = lax.ppermute(slots[1], "ctx", X_UP)
    slots[2] = lax.ppermute(slots[2], "ctx", X_TWO)
    slots[3] = lax.ppermute(slots[3], "ctx", X_DOWN)
    before = [b0, c0, b1, c1, b2, c2]
    give = attend_last(info, other_q, 1, before, [b4, c4], state[2:], "attend_give")
    slots, give = lax.optimization_barrier((slots, give))
    other = lax.ppermute(give, "ctx", Y_SWAP)
    keep, send = part_rows(slots, 4, "part_y")
    got = lax.ppermute(send, "ctx", Y_SWAP)
    mine = attend_last(info, stretch_q, 0, before, [b4, c4], state[:2], "attend_keep")
    keep, got, mine = lax.optimization_barrier((keep, got, mine))
    new_a, send = part_rows([keep, got], 2, "part_core")
    new_b = lax.ppermute(send, "ctx", CORE_SWAP)

    counts = (TOK, ctx_count * MOST, dec_q.shape[0])
    rows = sum(counts)
    above_far, below_far, cross, attn = project(
        project_first_kernel, (at_place, orders[0]), (mine, other, new_a, new_b, dec_attn), out_weight, rows,
        (TOK + 32 + 16, out_weight.shape[0]), VMEM_LIMIT, "project_far",
    )
    above_far = lax.ppermute(above_far, "tp", Z_UP)
    below_far = lax.ppermute(below_far, "tp", Z_DOWN)
    cross = lax.ppermute(cross, "tp", H_SWAP)
    above, below, across, two, own = project(
        project_rest_kernel, (orders[1],), (attn,), out_weight, rows, None, VMEM_LIMIT, "project_near"
    )
    above, below, above_far, below_far = lax.optimization_barrier((above, below, above_far, below_far))
    above = lax.ppermute(above, "tp", Z_UP)
    below = lax.ppermute(below, "tp", Z_DOWN)
    (across,) = add_up([across, above_far, below_far], (rows,), "add_far", 10**10)
    across = lax.ppermute(across, "tp", H_SWAP)
    two = lax.ppermute(total_of(two, cross), "tp", Z_TWO)
    stretch_out, new_out, dec_out = add_up([own, above, below, two, across], counts, "add_up", 0)
    return stretch_out, dec_out, new_out


def solution(mesh):
    in_specs = (
        P(),
        P("ctx", "tp"),
        P("ctx", "tp"),
        P("ctx", "tp"),
        P("ctx", "tp"),
        P("ctx", "tp"),
        P("ctx"),
        P("ctx", "tp"),
        P("ctx", "tp"),
        P("ctx", "tp"),
        P("ctx", None, "tp"),
        P("ctx", None, "tp"),
        P("ctx", None),
        P("ctx"),
        P("ctx", "tp"),
        P("ctx", None, "tp"),
        P("ctx", None, "tp"),
        P("tp", None),
    )
    out_specs = (P("ctx", "tp"), P("ctx", "tp"), P("ctx", "tp"))
    return jax.shard_map(local, mesh=mesh, in_specs=in_specs, out_specs=out_specs, check_vma=False)
```

```python
import functools
import math

import jax
import jax.numpy as jnp
from jax import lax
from jax.experimental import pallas as pl
from jax.experimental.pallas import tpu as pltpu
from jax.sharding import PartitionSpec as P

HEAD_DIM = 128
MOST = 2
GROUP = 8
TOK = 128
PRE = 1024
BLOCK = PRE + TOK
ROWS = GROUP * TOK
TILE = 512
SUB = 256
NEG = -1e30
SCALE = math.log2(math.e) / math.sqrt(HEAD_DIM)
LOW, HIGH = 2.0**-60, 2.0**100
VMEM_LIMIT = 24 * 2**20
STATS = 32


def dot_t(a, b):
    return lax.dot_general(a, b, (((1,), (1,)), ((), ())), preferred_element_type=jnp.float32)


def dot(a, b):
    return jnp.dot(a, b, preferred_element_type=jnp.float32)


def ctx_index(y, x, c):
    return y * 8 + x * 2 + c


def ctx_perm(move):
    return [
        (ctx_index(y, x, c), ctx_index(*move(y, x, c)))
        for y in range(2)
        for x in range(4)
        for c in range(2)
    ]


X_UP = ctx_perm(lambda y, x, c: (y, (x + 1) % 4, c))
X_DOWN = ctx_perm(lambda y, x, c: (y, (x + 3) % 4, c))
X_TWO = ctx_perm(lambda y, x, c: (y, (x + 2) % 4, c))
Y_SWAP = ctx_perm(lambda y, x, c: (1 - y, x, c))
CORE_SWAP = ctx_perm(lambda y, x, c: (y, x, 1 - c))


def tp_index(h, z):
    return h * 4 + z % 4


def tp_perm(move):
    return [(tp_index(h, z), tp_index(*move(h, z))) for h in range(2) for z in range(4)]


Z_UP = tp_perm(lambda h, z: (h, z + 1))
Z_DOWN = tp_perm(lambda h, z: (h, z + 3))
Z_TWO = tp_perm(lambda h, z: (h, z + 2))
H_SWAP = tp_perm(lambda h, z: (1 - h, z))


def lane_sums(p):
    total = p[:, 0:128]
    for at in range(128, p.shape[1], 128):
        total = total + p[:, at : at + 128]
    return total


def stack_queries(q_refs, queries):
    for half, ref in enumerate(q_refs):
        for head in range(GROUP):
            queries[pl.ds(half * ROWS + head * TOK, TOK), :] = ref[:, pl.ds(head * HEAD_DIM, HEAD_DIM)]


def add_block(info, block_at, kv, queries, acc, sums, halves):
    prefix_end = info[0]
    chunk = info[3 + block_at]
    count = jnp.clip(prefix_end - chunk * PRE, 0, PRE)

    @pl.when(count == PRE)
    def _():
        for tile in range(len(halves) * ROWS // TILE):
            rows = pl.ds(tile * TILE, TILE)
            for at in range(0, PRE, 512):
                p = jnp.exp2(dot_t(queries[rows, :], kv[pl.ds(at, 512), :]) * SCALE)
                acc[rows, :] += dot(p.astype(jnp.bfloat16), kv[pl.ds(BLOCK + at, 512), :])
                sums[rows, :] += lane_sums(p)

    @pl.when(jnp.logical_and(count > 0, count < PRE))
    def _():
        def step(at, carry):
            start = pl.multiple_of(at * SUB, SUB)
            columns = start + lax.broadcasted_iota(jnp.int32, (TILE, SUB), 1)
            for tile in range(len(halves) * ROWS // TILE):
                rows = pl.ds(tile * TILE, TILE)
                s = dot_t(queries[rows, :], kv[pl.ds(start, SUB), :]) * SCALE
                p = jnp.where(columns < count, jnp.exp2(s), 0.0)
                acc[rows, :] += dot(p.astype(jnp.bfloat16), kv[pl.ds(BLOCK + start, SUB), :])
                sums[rows, :] += lane_sums(p)
            return carry

        lax.fori_loop(0, (count + SUB - 1) // SUB, step, 0)


def add_tokens(info, first_block, kvs, queries, acc, sums, halves, near):
    count = len(kvs)
    width = count * TOK
    for at, kv in enumerate(kvs):
        near[pl.ds(at * TOK, TOK), :] = kv[pl.ds(PRE, TOK), :]
        near[pl.ds(width + at * TOK, TOK), :] = kv[pl.ds(BLOCK + PRE, TOK), :]
    for at_half, half in enumerate(halves):
        place = info[1 + half]
        seen_from = [place - info[3 + first_block + at] for at in range(count)]
        some = functools.reduce(jnp.maximum, seen_from)

        @pl.when(some >= 0)
        def _():
            column = lax.broadcasted_iota(jnp.int32, (1, width), 1)
            start = jnp.zeros((1, width), jnp.int32)
            for at in range(count):
                least = jnp.where(seen_from[at] > 0, -TOK, jnp.where(seen_from[at] == 0, 0, TOK))
                start = jnp.where(column // TOK == at, least, start)
            start = start + column % TOK
            token = lax.broadcasted_iota(jnp.int32, (TILE, width), 0) % TOK
            seen = start <= token
            for tile in range(ROWS // TILE):
                rows = pl.ds(at_half * ROWS + tile * TILE, TILE)
                s = dot_t(queries[rows, :], near[pl.ds(0, width), :]) * SCALE
                p = jnp.where(seen, jnp.exp2(s), 0.0)
                acc[rows, :] += dot(p.astype(jnp.bfloat16), near[pl.ds(width, width), :])
                sums[rows, :] += lane_sums(p)


def shifted_step(rows, s, seen, values, queries, acc, sums, peak):
    s = jnp.where(seen, s, NEG)
    before = peak[rows, :]
    now = jnp.maximum(before, jnp.max(s, axis=1, keepdims=True))
    p = jnp.where(seen, jnp.exp2(s - now[:, 0:1]), 0.0)
    fade = jnp.exp2(before - now)
    acc[rows, :] = acc[rows, :] * fade + dot(p.astype(jnp.bfloat16), values)
    sums[rows, :] = sums[rows, :] * fade + lane_sums(p)
    peak[rows, :] = now


def shifted_block(info, chunk, place, kv, queries, acc, sums, peak):
    count = jnp.clip(info[0] - chunk * PRE, 0, PRE)
    tile_rows = 256

    def tile_step(tile, carry):
        rows = pl.ds(pl.multiple_of(tile * tile_rows, tile_rows), tile_rows)

        def step(at, carry):
            start = pl.multiple_of(at * SUB, SUB)
            columns = start + lax.broadcasted_iota(jnp.int32, (tile_rows, SUB), 1)
            s = dot_t(queries[rows, :], kv[pl.ds(start, SUB), :]) * SCALE
            shifted_step(rows, s, columns < count, kv[pl.ds(BLOCK + start, SUB), :], queries, acc, sums, peak)
            return carry

        lax.fori_loop(0, (count + SUB - 1) // SUB, step, 0)

        @pl.when(chunk <= place)
        def _():
            token = lax.broadcasted_iota(jnp.int32, (tile_rows, TOK), 0) % TOK
            key = lax.broadcasted_iota(jnp.int32, (tile_rows, TOK), 1)
            seen = key <= token + jnp.where(chunk < place, TOK, 0)
            s = dot_t(queries[rows, :], kv[pl.ds(PRE, TOK), :]) * SCALE
            shifted_step(rows, s, seen, kv[pl.ds(BLOCK + PRE, TOK), :], queries, acc, sums, peak)

        return carry

    lax.fori_loop(0, ROWS // tile_rows, tile_step, 0)


def attend_kernel(halves, first_block, blocks, starts, info, *refs):
    count = len(halves)
    q_refs, refs = refs[:count], refs[count:]
    kvs, refs = refs[:blocks], refs[blocks:]
    if not starts:
        before, refs = refs[: 2 * count], refs[2 * count :]
    after, (queries, acc, sums, near) = refs[: 2 * count], refs[2 * count :]
    stack_queries(q_refs, queries)
    if starts:
        acc[...] = jnp.zeros_like(acc)
        sums[...] = jnp.zeros_like(sums)
    else:
        for at in range(count):
            acc[pl.ds(at * ROWS, ROWS), :] = before[2 * at][...]
            sums[pl.ds(at * ROWS, ROWS), :] = before[2 * at + 1][...]
    for at in range(blocks):
        add_block(info, first_block + at, kvs[at], queries, acc, sums, halves)
    add_tokens(info, first_block, kvs, queries, acc, sums, halves, near)
    for at in range(count):
        after[2 * at][...] = acc[pl.ds(at * ROWS, ROWS), :]
        after[2 * at + 1][...] = sums[pl.ds(at * ROWS, ROWS), :]


def last_kernel(half, earlier, blocks, info, q_ref, *refs):
    earlier_kvs, refs = refs[:earlier], refs[earlier:]
    kvs, refs = refs[:blocks], refs[blocks:]
    acc_in, sums_in, out, queries, acc, sums, near, peak, held, levels, sem = refs
    stack_queries((q_ref,), queries)
    acc[...] = acc_in[...]
    sums[...] = sums_in[...]
    for at in range(blocks):
        add_block(info, earlier + at, kvs[at], queries, acc, sums, (half,))
    add_tokens(info, earlier, kvs, queries, acc, sums, (half,), near)
    peak[...] = jnp.zeros_like(peak)
    has_keys = jnp.int32(0)
    for at in range(earlier + blocks):
        chunk = info[3 + at]
        some = jnp.logical_or(info[0] > chunk * PRE, chunk <= info[1 + half])
        has_keys = jnp.where(some, 1, has_keys)
    total = jnp.sum(sums[...], axis=1, keepdims=True)
    inside = jnp.where(jnp.logical_and(total >= LOW, total <= HIGH), 1.0, 0.0)

    @pl.when(jnp.logical_and(has_keys > 0, jnp.min(inside) < 0.5))
    def _():
        acc[...] = jnp.zeros_like(acc)
        sums[...] = jnp.zeros_like(sums)
        peak[...] = jnp.full_like(peak, NEG)

        def block_step(at, carry):
            for one in range(earlier + blocks):
                source = earlier_kvs[one] if one < earlier else kvs[one - earlier]

                @pl.when(at == one)
                def _():
                    copy = pltpu.make_async_copy(source, held, sem)
                    copy.start()
                    copy.wait()

            shifted_block(info, info[3 + at], info[1 + half], held, queries, acc, sums, peak)
            return carry

        lax.fori_loop(0, earlier + blocks, block_step, 0)

    for head in range(GROUP):
        rows = pl.ds(head * TOK, TOK)
        total = jnp.sum(sums[rows, :], axis=1, keepdims=True)
        out[rows, :] = (acc[rows, :] / jnp.where(total > 0, total, 1.0)).astype(out.dtype)
        level = jnp.where(total > 0, peak[rows, :] + jnp.log2(jnp.where(total > 0, total, 1.0)), NEG)
        levels[pl.ds(head, 1), :] = jnp.transpose(level)[0:1, :]
    high = levels[...].astype(jnp.bfloat16)
    rest = levels[...] - high.astype(jnp.float32)
    middle = rest.astype(jnp.bfloat16)
    low = (rest - middle.astype(jnp.float32)).astype(jnp.bfloat16)
    out[pl.ds(ROWS, STATS), :] = jnp.concatenate([high, middle, low, jnp.zeros_like(low)], 0)


def unpack_levels(packed):
    pieces = [packed[pl.ds(ROWS, STATS), :].astype(jnp.float32)]
    return pieces[0][0:8] + pieces[0][8:16] + pieces[0][16:24]


def whole(shape):
    return pl.BlockSpec(shape, lambda *_: (0,) * len(shape))


SMEM = pl.BlockSpec(memory_space=pltpu.SMEM)
STATE = jax.ShapeDtypeStruct((ROWS, 128), jnp.float32)


def attend_cost(halves, blocks):
    return pl.CostEstimate(
        flops=blocks * 4 * halves * ROWS * BLOCK * HEAD_DIM * 2,
        bytes_accessed=blocks * BLOCK * 512 + 4 * halves * ROWS * 512,
        transcendentals=blocks * halves * ROWS * BLOCK,
    )


def attend(info, queries, halves, first_block, kvs, state, name):
    blocks, count = len(kvs), len(halves)
    return pl.pallas_call(
        functools.partial(attend_kernel, halves, first_block, blocks, not state),
        out_shape=[STATE] * (2 * count),
        in_specs=[SMEM]
        + [whole(q.shape) for q in queries]
        + [whole(kv.shape) for kv in kvs]
        + [whole(STATE.shape)] * len(state),
        out_specs=[whole(STATE.shape)] * (2 * count),
        scratch_shapes=[
            pltpu.VMEM((count * ROWS, HEAD_DIM), jnp.bfloat16),
            pltpu.VMEM((count * ROWS, 128), jnp.float32),
            pltpu.VMEM((count * ROWS, 128), jnp.float32),
            pltpu.VMEM((2 * blocks * TOK, HEAD_DIM), jnp.bfloat16),
        ],
        compiler_params=pltpu.CompilerParams(vmem_limit_bytes=VMEM_LIMIT),
        cost_estimate=attend_cost(count, blocks),
        name=name,
    )(info, *queries, *kvs, *state)


def attend_last(info, q, half, earlier, kvs, state, name):
    blocks = len(kvs)
    packed = jax.ShapeDtypeStruct((ROWS + STATS, HEAD_DIM), jnp.bfloat16)
    return pl.pallas_call(
        functools.partial(last_kernel, half, len(earlier), blocks),
        grid=(1,),
        out_shape=packed,
        in_specs=[SMEM, whole(q.shape)]
        + [pl.BlockSpec(memory_space=pl.ANY)] * len(earlier)
        + [whole(kv.shape) for kv in kvs]
        + [whole(STATE.shape)] * 2,
        out_specs=whole(packed.shape),
        scratch_shapes=[
            pltpu.VMEM((ROWS, HEAD_DIM), jnp.bfloat16),
            pltpu.VMEM((ROWS, 128), jnp.float32),
            pltpu.VMEM((ROWS, 128), jnp.float32),
            pltpu.VMEM((2 * blocks * TOK, HEAD_DIM), jnp.bfloat16),
            pltpu.VMEM((ROWS, 128), jnp.float32),
            pltpu.VMEM((2 * BLOCK, HEAD_DIM), jnp.bfloat16),
            pltpu.VMEM((GROUP, TOK), jnp.float32),
            pltpu.SemaphoreType.DMA(()),
        ],
        compiler_params=pltpu.CompilerParams(vmem_limit_bytes=VMEM_LIMIT),
        cost_estimate=attend_cost(1, blocks),
        name=name,
    )(info, q, *earlier, *kvs, *state)


def softmax_rows(s, seen):
    s = jnp.where(seen, s, NEG)
    return s, jnp.max(s, axis=1, keepdims=True)


def spread(rows, flat):
    for head in range(GROUP):
        piece = rows[:, pl.ds(head * HEAD_DIM, HEAD_DIM)].astype(jnp.float32)
        flat[pl.ds(head, rows.shape[0], stride=GROUP), :] = piece


def gather_heads(flat, rows):
    for head in range(GROUP):
        piece = flat[pl.ds(head, rows.shape[0], stride=GROUP), :]
        rows[:, pl.ds(head * HEAD_DIM, HEAD_DIM)] = piece.astype(rows.dtype)


def heads_at(row):
    return pl.ds(pl.multiple_of(row * GROUP, GROUP), GROUP)


def relative(to, place):
    x_steps = (to // 2 - place // 2 + 4) % 4
    return x_steps * 4 + ((to // 8) ^ (place // 8)) * 2 + ((to % 2) ^ (place % 2))


def rows_kernel(
    dec_len, owner, hand_count, place, dec_q, dec_k, dec_v, hand_q, cache_k, cache_v, hand_k, hand_v,
    dec_out, slot_0, slot_1, slot_2, slot_3,
    dec_rows, hand_rows, dec_sums, slot_sums, cache_ks, cache_vs, hand_ks, hand_vs, sems, taken,
):
    rows, blocks = cache_k.shape[0], hand_k.shape[0]
    copies = [pltpu.make_async_copy(hand_k, hand_ks, sems.at[0]), pltpu.make_async_copy(hand_v, hand_vs, sems.at[1])]
    for row in range(rows):
        copies.append(pltpu.make_async_copy(cache_k.at[row], cache_ks.at[row], sems.at[2 + 2 * row]))
        copies.append(pltpu.make_async_copy(cache_v.at[row], cache_vs.at[row], sems.at[3 + 2 * row]))
    for copy in copies:
        copy.start()
    spread(dec_q, dec_rows)
    spread(hand_q, hand_rows)
    dec_sums[...] = jnp.zeros_like(dec_sums)
    slot_sums[...] = jnp.zeros_like(slot_sums)
    for at in range(taken.shape[0]):
        taken[at] = 0
    copies[0].wait()
    copies[1].wait()
    queries = [hand_rows[pl.ds(at * GROUP, GROUP), :].astype(jnp.bfloat16) for at in range(blocks)]
    s = jnp.concatenate([dot_t(queries[at], hand_ks[at]) for at in range(blocks)], 0) * SCALE
    count = jnp.zeros(s.shape, jnp.int32)
    block_of = lax.broadcasted_iota(jnp.int32, s.shape, 0) // GROUP
    for at in range(blocks):
        count = jnp.where(block_of == at, hand_count[at], count)
    seen = lax.broadcasted_iota(jnp.int32, s.shape, 1) < count
    s, top = softmax_rows(s, seen)
    p = jnp.where(seen, jnp.exp2(s - top), 0.0)
    total = jnp.sum(p, axis=1, keepdims=True)
    summed = [
        dot(p[at * GROUP : (at + 1) * GROUP].astype(jnp.bfloat16), hand_vs[at]) for at in range(blocks)
    ]
    results = jnp.concatenate(summed, 0) / jnp.where(total > 0, total, 1.0)
    for at in range(blocks):
        to = owner[at]
        slot = relative(to, place[0]) * MOST + taken[to]
        taken[to] = taken[to] + 1
        slot_sums[heads_at(slot), :] = results[at * GROUP : (at + 1) * GROUP]
    for copy in copies[2:]:
        copy.wait()
    queries = [dec_rows[pl.ds(row * GROUP, GROUP), :].astype(jnp.bfloat16) for row in range(rows)]
    s = jnp.concatenate([dot_t(queries[row], cache_ks[row]) for row in range(rows)], 0) * SCALE
    keys = jnp.concatenate(
        [jnp.broadcast_to(dec_k[row : row + 1, :].astype(jnp.float32), (GROUP, HEAD_DIM)) for row in range(rows)], 0
    )
    values = jnp.concatenate(
        [jnp.broadcast_to(dec_v[row : row + 1, :].astype(jnp.float32), (GROUP, HEAD_DIM)) for row in range(rows)], 0
    )
    own = jnp.sum(dec_rows[...] * keys, axis=1, keepdims=True) * SCALE
    row_of = lax.broadcasted_iota(jnp.int32, (rows * GROUP, 1), 0) // GROUP
    count = jnp.zeros((rows * GROUP, 1), jnp.int32)
    for row in range(rows):
        count = jnp.where(row_of == row, dec_len[row], count)
    seen = lax.broadcasted_iota(jnp.int32, s.shape, 1) < count
    s, top = softmax_rows(s, seen)
    top = jnp.maximum(top, own)
    p = jnp.where(seen, jnp.exp2(s - top), 0.0)
    own = jnp.exp2(own - top)
    total = jnp.sum(p, axis=1, keepdims=True) + own
    p = p.astype(jnp.bfloat16)
    summed = jnp.concatenate([dot(p[row * GROUP : (row + 1) * GROUP], cache_vs[row]) for row in range(rows)], 0)
    summed = summed + own.astype(jnp.bfloat16).astype(jnp.float32) * values
    dec_sums[pl.ds(0, rows * GROUP), :] = summed / total
    gather_heads(dec_sums, dec_out)
    for step, out in enumerate((slot_0, slot_1, slot_2, slot_3)):
        gather_heads(slot_sums.at[pl.ds(step * 8 * GROUP, 8 * GROUP)], out)


def attend_rows(dec_len, owner, hand_count, place, dec_q, dec_k, dec_v, hand_q, cache_k, cache_v, hand_k, hand_v, owners):
    rows = cache_k.shape[0]
    blocks = hand_k.shape[0]
    width = dec_q.shape[1]
    return pl.pallas_call(
        rows_kernel,
        out_shape=(
            jax.ShapeDtypeStruct((16, width), jnp.bfloat16),
            *[jax.ShapeDtypeStruct((owners * MOST // 4, width), jnp.float32)] * 4,
        ),
        in_specs=[SMEM] * 4
        + [whole(a.shape) for a in (dec_q, dec_k, dec_v, hand_q)]
        + [pl.BlockSpec(memory_space=pl.ANY)] * 4,
        out_specs=(whole((16, width)), *[whole((owners * MOST // 4, width))] * 4),
        scratch_shapes=[
            pltpu.VMEM((rows * GROUP, HEAD_DIM), jnp.float32),
            pltpu.VMEM((blocks * GROUP, HEAD_DIM), jnp.float32),
            pltpu.VMEM((16 * GROUP, HEAD_DIM), jnp.float32),
            pltpu.VMEM((owners * MOST * GROUP, HEAD_DIM), jnp.float32),
            pltpu.VMEM(cache_k.shape, jnp.bfloat16),
            pltpu.VMEM(cache_v.shape, jnp.bfloat16),
            pltpu.VMEM(hand_k.shape, jnp.bfloat16),
            pltpu.VMEM(hand_v.shape, jnp.bfloat16),
            pltpu.SemaphoreType.DMA((2 + 2 * rows,)),
            pltpu.SMEM((owners,), jnp.int32),
        ],
        compiler_params=pltpu.CompilerParams(vmem_limit_bytes=56 * 2**20),
        cost_estimate=pl.CostEstimate(flops=10**6, bytes_accessed=10**4, transcendentals=0),
        name="rows",
    )(dec_len, owner, hand_count, place, dec_q, dec_k, dec_v, hand_q, cache_k, cache_v, hand_k, hand_v)


def part_kernel(count, rows, *refs):
    pieces, (keep, send) = refs[:count], refs[count:]
    at = 0
    for piece in pieces:
        for start in range(0, piece.shape[0], 2 * rows):
            keep[pl.ds(at, rows), :] = piece[pl.ds(start, rows), :]
            send[pl.ds(at, rows), :] = piece[pl.ds(start + rows, rows), :]
            at += rows


def part_rows(pieces, rows, name):
    half = sum(piece.shape[0] for piece in pieces) // 2
    out = jax.ShapeDtypeStruct((half, pieces[0].shape[1]), pieces[0].dtype)
    return pl.pallas_call(
        functools.partial(part_kernel, len(pieces), rows),
        out_shape=(out, out),
        in_specs=[whole(piece.shape) for piece in pieces],
        out_specs=(whole(out.shape),) * 2,
        compiler_params=pltpu.CompilerParams(vmem_limit_bytes=8 * 2**20),
        name=name,
    )(*pieces)


def join_kernel(*refs):
    sources, out, sems = refs[:4], refs[4], refs[5]
    copies = []
    at = 0
    for n, source in enumerate(sources):
        copies.append(pltpu.make_async_copy(source, out.at[pl.ds(at, source.shape[0])], sems.at[n]))
        at += source.shape[0]
    for copy in copies:
        copy.start()
    for copy in copies:
        copy.wait()


def join(*pieces):
    rows = sum(piece.shape[0] for piece in pieces)
    return pl.pallas_call(
        join_kernel,
        out_shape=jax.ShapeDtypeStruct((rows, HEAD_DIM), jnp.bfloat16),
        in_specs=[pl.BlockSpec(memory_space=pl.ANY)] * 4,
        out_specs=whole((rows, HEAD_DIM)),
        scratch_shapes=[pltpu.SemaphoreType.DMA((4,))],
        compiler_params=pltpu.CompilerParams(vmem_limit_bytes=56 * 2**20),
        cost_estimate=pl.CostEstimate(flops=0, bytes_accessed=rows * 512, transcendentals=0),
        name="join",
    )(*pieces)


def column(row):
    return jnp.transpose(jnp.broadcast_to(row, (TOK, TOK)))


def slot_order(place):
    count = 32
    to = lax.broadcasted_iota(jnp.int32, (count, count), 0)
    at = lax.broadcasted_iota(jnp.int32, (count, count), 1)
    core, high, steps, rank = at // 16, (at // 8) % 2, (at // 2) % 4, at % 2
    x = (place // 2 - steps + 4) % 4
    source = ((place // 8) ^ high) * 8 + x * 2 + ((place % 2) ^ core)
    return jnp.where(to == source * 2 + rank, 1.0, 0.0).astype(jnp.bfloat16)


def project_first_kernel(place, order, mine, other, new_a, new_b, dec, weight, *refs):
    outs, attn = refs[:-1], refs[-1]

    @pl.when(pl.program_id(0) == 0)
    def _():
        a_levels, b_levels = unpack_levels(mine), unpack_levels(other)
        top = jnp.maximum(a_levels, b_levels)
        wa, wb = jnp.exp2(a_levels - top), jnp.exp2(b_levels - top)
        wa, wb = wa / (wa + wb), wb / (wa + wb)
        for head in range(GROUP):
            rows = pl.ds(head * TOK, TOK)
            a, b = mine[rows, :].astype(jnp.float32), other[rows, :].astype(jnp.float32)
            mixed = a * column(wa[head : head + 1, :]) + b * column(wb[head : head + 1, :])
            attn[pl.ds(0, TOK), pl.ds(head * HEAD_DIM, HEAD_DIM)] = mixed.astype(attn.dtype)
        new = jnp.concatenate([new_a[...], new_b[...]], 0).astype(jnp.bfloat16)
        attn[pl.ds(TOK, 32), :] = dot(slot_order(place[0]), new).astype(attn.dtype)
        attn[pl.ds(TOK + 32, 16), :] = dec[...]

    project_step(outs, attn, weight)


def project_rest_kernel(order, attn, weight, *outs):
    project_step(outs, attn, weight)


def project_step(outs, attn, weight):
    result = dot(attn[...], weight[...]).astype(jnp.bfloat16)
    for step, out in enumerate(outs):

        @pl.when(pl.program_id(0) == step)
        def _():
            out[...] = result[: out.shape[0]]


def project(kernel, scalars, inputs, weight, rows, attn_shape, vmem, name):
    depth, width = weight.shape
    steps = scalars[-1].shape[0]
    columns = 1024
    outs = [jax.ShapeDtypeStruct((rows, columns), jnp.bfloat16)] * steps
    if attn_shape:
        outs.append(jax.ShapeDtypeStruct(attn_shape, jnp.bfloat16))
    return pl.pallas_call(
        kernel,
        grid_spec=pltpu.PrefetchScalarGridSpec(
            num_scalar_prefetch=len(scalars),
            grid=(steps,),
            in_specs=[whole(a.shape) for a in inputs]
            + [pl.BlockSpec((depth, columns), lambda i, *scalars: (0, scalars[-1][i]))],
            out_specs=[whole(out.shape) for out in outs],
        ),
        out_shape=outs,
        compiler_params=pltpu.CompilerParams(vmem_limit_bytes=vmem),
        cost_estimate=pl.CostEstimate(
            flops=2 * rows * depth * columns * steps, bytes_accessed=2 * depth * columns * steps, transcendentals=0
        ),
        name=name,
    )(*scalars, *inputs, weight)


def total_of(*parts):
    total = parts[0].astype(jnp.float32)
    for part in parts[1:]:
        total = total + part.astype(jnp.float32)
    return total.astype(jnp.bfloat16)


def total_kernel(count, *refs):
    parts, outs = refs[:count], refs[count:]
    total = parts[0][...].astype(jnp.float32)
    for part in parts[1:]:
        total = total + part[...].astype(jnp.float32)
    total = total.astype(jnp.bfloat16)
    at = 0
    for out in outs:
        out[...] = total[at : at + out.shape[0]]
        at += out.shape[0]


def add_up(parts, rows, name, flops):
    width = parts[0].shape[1]
    return pl.pallas_call(
        functools.partial(total_kernel, len(parts)),
        out_shape=[jax.ShapeDtypeStruct((count, width), jnp.bfloat16) for count in rows],
        in_specs=[whole(part.shape) for part in parts],
        out_specs=[whole((count, width)) for count in rows],
        compiler_params=pltpu.CompilerParams(vmem_limit_bytes=VMEM_LIMIT),
        cost_estimate=pl.CostEstimate(flops=flops, bytes_accessed=len(parts) * sum(rows) * width * 2, transcendentals=0),
        name=name,
    )(*parts)


def local(
    stretch_start,
    stretch_q,
    stretch_k,
    stretch_v,
    prefix_k,
    prefix_v,
    dec_len,
    dec_q,
    dec_k,
    dec_v,
    cache_k,
    cache_v,
    hand_owner,
    hand_count,
    hand_q,
    hand_k,
    hand_v,
    out_weight,
):
    place = lax.axis_index("ctx")
    me = lax.axis_index("tp")
    y, x, c = place // 8, (place // 2) % 4, place % 2

    b0 = join(prefix_k, stretch_k, prefix_v, stretch_v)
    b1 = lax.ppermute(b0, "ctx", X_UP)
    b2 = lax.ppermute(b0, "ctx", X_DOWN)
    c0 = lax.ppermute(b0, "ctx", CORE_SWAP)
    other_q = lax.ppermute(stretch_q, "ctx", Y_SWAP)
    up, down, two = (x + 1) % 4, (x + 3) % 4, (x + 2) % 4
    info = jnp.stack(
        [
            stretch_start[0],
            place,
            ctx_index(1 - y, x, c),
            place,
            ctx_index(y, x, 1 - c),
            ctx_index(y, down, c),
            ctx_index(y, down, 1 - c),
            ctx_index(y, up, c),
            ctx_index(y, up, 1 - c),
            ctx_index(y, two, c),
            ctx_index(y, two, 1 - c),
        ]
    ).astype(jnp.int32)

    h, z = me // 4, me % 4
    order_far = jnp.stack([tp_index(1 - h, z + 1), tp_index(1 - h, z + 3), tp_index(1 - h, z + 2)]).astype(jnp.int32)
    order_near = jnp.stack([tp_index(h, z + 1), tp_index(h, z + 3)]).astype(jnp.int32)
    order_rest = jnp.stack([tp_index(1 - h, z), tp_index(h, z + 2), me]).astype(jnp.int32)
    orders = (order_far, order_near, order_rest)
    ctx_count = lax.axis_size("ctx")
    at_place = place[None].astype(jnp.int32)
    info, orders, at_place = lax.optimization_barrier((info, orders, at_place))
    dec_attn, *slots = attend_rows(
        dec_len, hand_owner[:, 0], hand_count, at_place, dec_q, dec_k, dec_v, hand_q,
        cache_k, cache_v, hand_k, hand_v, ctx_count,
    )
    info, orders, other_q, dec_attn = lax.optimization_barrier((info, orders, other_q, dec_attn))
    state = attend(info, [stretch_q, other_q], (0, 1), 0, [b0, c0], [], "attend_first")
    info, b0_later, b1, b2, state = lax.optimization_barrier((info, b0, b1, b2, state))
    b4 = lax.ppermute(b0_later, "ctx", X_TWO)
    c1 = lax.ppermute(b1, "ctx", CORE_SWAP)
    c2 = lax.ppermute(b2, "ctx", CORE_SWAP)

    state = attend(info, [stretch_q, other_q], (0, 1), 2, [b1, c1, b2, c2], state, "attend_both")

    slots, state, b4 = lax.optimization_barrier((slots, state, b4))
    c4 = lax.ppermute(b4, "ctx", CORE_SWAP)
    slots[1] = lax.ppermute(slots[1], "ctx", X_UP)
    slots[2] = lax.ppermute(slots[2], "ctx", X_TWO)
    slots[3] = lax.ppermute(slots[3], "ctx", X_DOWN)
    before = [b0, c0, b1, c1, b2, c2]
    give = attend_last(info, other_q, 1, before, [b4, c4], state[2:], "attend_give")
    slots, give = lax.optimization_barrier((slots, give))
    other = lax.ppermute(give, "ctx", Y_SWAP)
    keep, send = part_rows(slots, 4, "part_y")
    got = lax.ppermute(send, "ctx", Y_SWAP)
    mine = attend_last(info, stretch_q, 0, before, [b4, c4], state[:2], "attend_keep")
    keep, got, mine = lax.optimization_barrier((keep, got, mine))
    new_a, send = part_rows([keep, got], 2, "part_core")
    new_b = lax.ppermute(send, "ctx", CORE_SWAP)

    counts = (TOK, ctx_count * MOST, dec_q.shape[0])
    rows = sum(counts)
    above_far, below_far, cross, attn = project(
        project_first_kernel, (at_place, orders[0]), (mine, other, new_a, new_b, dec_attn), out_weight, rows,
        (TOK + 32 + 16, out_weight.shape[0]), VMEM_LIMIT, "project_far",
    )
    above_far = lax.ppermute(above_far, "tp", Z_UP)
    below_far = lax.ppermute(below_far, "tp", Z_DOWN)
    cross = lax.ppermute(cross, "tp", H_SWAP)
    above, below = project(
        project_rest_kernel, (orders[1],), (attn,), out_weight, rows, None, VMEM_LIMIT, "project_near"
    )
    across, two, own = project(
        project_rest_kernel, (orders[2],), (attn,), out_weight, rows, None, VMEM_LIMIT, "project_rest"
    )
    above, below, above_far, below_far = lax.optimization_barrier((above, below, above_far, below_far))
    above = lax.ppermute(above, "tp", Z_UP)
    below = lax.ppermute(below, "tp", Z_DOWN)
    (across,) = add_up([across, above_far, below_far], (rows,), "add_far", 10**10)
    across = lax.ppermute(across, "tp", H_SWAP)
    two = lax.ppermute(total_of(two, cross), "tp", Z_TWO)
    stretch_out, new_out, dec_out = add_up([own, above, below, two, across], counts, "add_up", 0)
    return stretch_out, dec_out, new_out


def solution(mesh):
    in_specs = (
        P(),
        P("ctx", "tp"),
        P("ctx", "tp"),
        P("ctx", "tp"),
        P("ctx", "tp"),
        P("ctx", "tp"),
        P("ctx"),
        P("ctx", "tp"),
        P("ctx", "tp"),
        P("ctx", "tp"),
        P("ctx", None, "tp"),
        P("ctx", None, "tp"),
        P("ctx", None),
        P("ctx"),
        P("ctx", "tp"),
        P("ctx", None, "tp"),
        P("ctx", None, "tp"),
        P("tp", None),
    )
    out_specs = (P("ctx", "tp"), P("ctx", "tp"), P("ctx", "tp"))
    return jax.shard_map(local, mesh=mesh, in_specs=in_specs, out_specs=out_specs, check_vma=False)
```
